32 devices in a mesh: gz: 4 (over x, core), subj: 8 (over z, y).
Axes of the slice: x: 2, y: 2, z: 4, core: 2. Of those that a mesh axis runs over, the one named last changes fastest.
Arguments:
- template: bfloat16 [256, 8, 128], P(('gz', 'subj')), may hold values from -6 to 6
- subjects: bfloat16 [8, 256, 8, 128], P('subj', 'gz'), may hold values from -6 to 6
- shifts: int32 [8, 3, 256, 8, 128], P('subj', None, 'gz'), may hold values from -2 to 2
- fractions: bfloat16 [8, 3, 256, 8, 128], P('subj', None, 'gz'), may hold values from 0 to 1
Outputs:
- velocity_step: float32 [8, 3, 256, 8, 128], P('subj', None, 'gz')
- template_force: float32 [256, 8, 128], P(('gz', 'subj'))
The draws below stay inside these ranges and needn't reach their ends.
All inputs are finite; a program needn't handle non-finite values.
Results may differ from the reference program's by a relative error of at most 0.0029.
Values may be sent and summed in bfloat16 or wider, within the bound.
No kernel may reach another device: no remote copies, remote signals or barrier semaphores. Data moves between devices by JAX's collectives and lax.ppermute only.
A program may use at most 64 MiB of HBM per device.

```python
import math
import jax
import jax.numpy as jnp
from jax import lax

X = 8
Y = 128
SHIFT = 2
WIN = 4
SMOOTH = 4
SUBJECTS = 8
NZ = 256


def plant(result, own_key, least, top_value):
    shape = result.shape
    spot = [jax.random.randint(jax.random.fold_in(own_key, axis), (), 0, shape[axis]) for axis in range(len(shape))]
    result = result.at[tuple(spot)].set(least)
    longest = shape.index(max(shape))
    spot[longest] = (spot[longest] + 1) % shape[longest]
    return result.at[tuple(spot)].set(top_value)


def strengthened(entries, own_key, source, target, shards_of, factor):
    owner, partner = [(jnp.arange(entries.shape[dim]) // (entries.shape[dim] // shards_of)).reshape([-1 if axis == dim else 1 for axis in range(entries.ndim)]) for dim in (source, target)]
    chosen = jax.random.permutation(own_key, shards_of)[partner]
    strong = (owner == chosen) | (owner == (partner + shards_of // 2) % shards_of)
    return jnp.where(strong, factor * entries, entries)


def steps_of(key, shape, pieces, least, top_value):
    def one(dim, blocks):
        heights = jax.random.uniform(jax.random.fold_in(jax.random.fold_in(key, 6), dim), (blocks,), jnp.float32, least / len(pieces), top_value / len(pieces))
        return jnp.repeat(jnp.exp(heights), shape[dim] // blocks).reshape((-1,) + (1,) * (len(shape) - dim - 1))

    level = one(*pieces[0])
    for cut in pieces[1:]:
        level = level * one(*cut)
    return level


def bell_draw(own_key, shape, scale, most, shards=(), kind=jnp.bfloat16):
    level = steps_of(own_key, shape, shards, -0.22, 0.18) if shards else 1.0
    result = jax.random.normal(own_key, shape, jnp.float32) * scale * level
    return jnp.minimum(jnp.maximum(result, -most), most).astype(kind)


def gaussian_with(rng, extent, scale, limit, shards, heavy, kind=jnp.bfloat16):
    entries = scale * jax.random.normal(rng, extent, jnp.float32)
    if shards:
        entries = entries * steps_of(rng, extent, shards, -0.22, 0.18)
    return jnp.clip(strengthened(entries, jax.random.fold_in(rng, 3), *heavy), -limit, limit).astype(kind)


def setup_inputs(seed: int = 0) -> dict:
    splits = jax.random.split(jax.random.key(seed), 5)
    template = bell_draw(splits[0], (NZ, X, Y), 1.0, 6.0, ((0, 32),))
    subjects = gaussian_with(splits[1], (SUBJECTS, NZ, X, Y), 1.0, 6.0, ((0, 8), (1, 4)), (0, 1, 8, 2.0))
    shifts = plant(jax.random.randint(splits[2], (SUBJECTS, 3, NZ, X, Y), 0 - SHIFT, SHIFT + 1), jax.random.fold_in(splits[2], 1), 0 - SHIFT, SHIFT).astype(jnp.int32)
    fractions = jnp.clip(1.0 * jax.random.uniform(splits[3], (SUBJECTS, 3, NZ, X, Y), jnp.float32) ** steps_of(splits[3], (SUBJECTS, 3, NZ, X, Y), ((0, 8), (2, 4)), -0.2, 0.2), 0.0, 1.0).astype(jnp.bfloat16)
    return dict(template=template, subjects=subjects, shifts=shifts, fractions=fractions)


sigma = 1.5
epsilon = 1e-05
highest = lax.Precision.HIGHEST

def gauss_norm():
    offsets = jnp.arange(-SMOOTH, SMOOTH + 1, dtype=jnp.int32).astype(jnp.float32)
    return jnp.sum(jnp.exp(-0.5 * offsets * offsets / (sigma * sigma)))

def gauss_taps():
    offsets = jnp.arange(-SMOOTH, SMOOTH + 1, dtype=jnp.int32).astype(jnp.float32)
    return jnp.exp(-0.5 * offsets * offsets / (sigma * sigma)) / gauss_norm()

def band_matrix(length, radius):
    places = jnp.arange(length, dtype=jnp.int32)
    apart = places[:, None] - places[None, :]
    return (jnp.abs(apart) <= radius).astype(jnp.float32)

def gauss_matrix(length):
    places = jnp.arange(length, dtype=jnp.int32)
    apart = places[:, None] - places[None, :]
    offsets = apart.astype(jnp.float32)
    values = jnp.exp(-0.5 * offsets * offsets / (sigma * sigma)) / gauss_norm()
    return jnp.where(jnp.abs(apart) <= SMOOTH, values, jnp.zeros_like(values))

def inplane(fields, row_matrix, col_matrix):
    mixed = jnp.einsum('...xy,yv->...xv', fields, col_matrix, precision=highest)
    return jnp.einsum('...xy,xu->...uy', mixed, row_matrix, precision=highest)

def zwindow(fields, length, taps):
    summed = taps[0] * fields[..., 0:length, :, :]
    for offset in range(1, taps.shape[0]):
        summed = summed + taps[offset] * fields[..., offset:offset + length, :, :]
    return summed

def warp(padded_template, front, shift_one, frac_one):
    depth_len, row_len, col_len = frac_one.shape[1:]
    depth_index = jnp.arange(depth_len, dtype=jnp.int32)[:, None, None] + shift_one[0] + front
    row_index = jnp.arange(row_len, dtype=jnp.int32)[None, :, None] + shift_one[1] + SHIFT
    col_index = jnp.arange(col_len, dtype=jnp.int32)[None, None, :] + shift_one[2] + SHIFT
    flat_values = padded_template.reshape(-1)
    row_stride = padded_template.shape[1]
    col_stride = padded_template.shape[2]
    weights = frac_one.astype(jnp.float32)
    summed = jnp.zeros(frac_one.shape[1:], jnp.float32)
    for a in (0, 1):
        weight_depth = weights[0] if a else 1.0 - weights[0]
        for b in (0, 1):
            weight_row = weights[1] if b else 1.0 - weights[1]
            for e in (0, 1):
                weight_col = weights[2] if e else 1.0 - weights[2]
                position = ((depth_index + a) * row_stride + row_index + b) * col_stride + col_index + e
                summed = summed + weight_depth * weight_row * weight_col * jnp.take(flat_values, position)
    return lax.optimization_barrier(summed.astype(jnp.bfloat16))

def correlation_force(warped_ext, subject_ext, length):
    row_count = warped_ext.shape[-2]
    col_count = warped_ext.shape[-1]
    stacked = jnp.stack([warped_ext, subject_ext, warped_ext * warped_ext, subject_ext * subject_ext, warped_ext * subject_ext])
    box_sums = inplane(stacked, band_matrix(row_count, WIN), band_matrix(col_count, WIN))
    window = float((2 * WIN + 1) ** 3)
    local_means = zwindow(box_sums, length, jnp.ones((2 * WIN + 1,), jnp.float32)) / window
    centre_warped = warped_ext[..., WIN:WIN + length, :, :]
    centre_subject = subject_ext[..., WIN:WIN + length, :, :]
    var_warped = local_means[2] - local_means[0] * local_means[0]
    var_subject = local_means[3] - local_means[1] * local_means[1]
    covariance = local_means[4] - local_means[0] * local_means[1]
    factor = (centre_subject - local_means[1] - covariance / (var_warped + epsilon) * (centre_warped - local_means[0])) / jnp.sqrt(var_warped * var_subject + epsilon)
    grad_depth = 0.5 * (warped_ext[..., WIN + 1:WIN + 1 + length, :, :] - warped_ext[..., WIN - 1:WIN - 1 + length, :, :])
    padded = jnp.pad(centre_warped, [(0, 0)] * (centre_warped.ndim - 2) + [(1, 1), (1, 1)])
    grad_rows = 0.5 * (padded[..., 2:, 1:-1] - padded[..., :-2, 1:-1])
    grad_cols = 0.5 * (padded[..., 1:-1, 2:] - padded[..., 1:-1, :-2])
    return jnp.stack([factor * grad_depth, factor * grad_rows, factor * grad_cols], axis=-4)

def smooth(force_ext, length):
    along = zwindow(force_ext, length, gauss_taps())
    return inplane(along, gauss_matrix(force_ext.shape[-2]), gauss_matrix(force_ext.shape[-1]))

def reference(template, subjects, shifts, fractions):
    depth_len = template.shape[0]
    padded_template = jnp.pad(template.astype(jnp.float32), ((SHIFT, SHIFT + 1), (SHIFT, SHIFT + 1), (SHIFT, SHIFT + 1)))

    def one_subject(carried, inputs):
        image, shift_one, frac_one = inputs
        warped = warp(padded_template, SHIFT, shift_one, frac_one).astype(jnp.float32)
        image_f = image.astype(jnp.float32)
        depth_pad = ((WIN, WIN), (0, 0), (0, 0))
        force = correlation_force(jnp.pad(warped, depth_pad), jnp.pad(image_f, depth_pad), depth_len)
        force_ext = jnp.pad(force, ((0, 0), (SMOOTH, SMOOTH), (0, 0), (0, 0)))
        return (carried + (image_f - warped), smooth(force_ext, depth_len))
    residual, velocity = lax.scan(one_subject, jnp.zeros(template.shape, jnp.float32), (subjects, shifts, fractions))
    return (velocity, residual * (1.0 / math.sqrt(SUBJECTS)))
```

```python
import math

import jax
import jax.numpy as jnp
from jax import lax
from jax.sharding import PartitionSpec as P

SHIFT = 2
WIN = 4
SMOOTH = 4


sigma = 1.5
epsilon = 1e-05
highest = lax.Precision.HIGHEST


def with_halo(block, sides, width):
    for axis, dim in sides:
        count = lax.axis_size(axis)
        forward = [(i, i + 1) for i in range(count - 1)]
        backward = [(target, source) for source, target in forward]
        low = lax.ppermute(
            lax.slice_in_dim(block, block.shape[dim] - width, None, axis=dim), axis, forward
        )
        high = lax.ppermute(lax.slice_in_dim(block, 0, width, axis=dim), axis, backward)
        block = jnp.concatenate([low, block, high], axis=dim)
    return block


def gauss_norm():
    offsets = jnp.arange(-SMOOTH, SMOOTH + 1, dtype=jnp.int32).astype(jnp.float32)
    return jnp.sum(jnp.exp(-0.5 * offsets * offsets / (sigma * sigma)))


def gauss_taps():
    offsets = jnp.arange(-SMOOTH, SMOOTH + 1, dtype=jnp.int32).astype(jnp.float32)
    return jnp.exp(-0.5 * offsets * offsets / (sigma * sigma)) / gauss_norm()


def band_matrix(length, radius):
    places = jnp.arange(length, dtype=jnp.int32)
    apart = places[:, None] - places[None, :]
    return (jnp.abs(apart) <= radius).astype(jnp.float32)


def gauss_matrix(length):
    places = jnp.arange(length, dtype=jnp.int32)
    apart = places[:, None] - places[None, :]
    offsets = apart.astype(jnp.float32)
    values = jnp.exp(-0.5 * offsets * offsets / (sigma * sigma)) / gauss_norm()
    return jnp.where(jnp.abs(apart) <= SMOOTH, values, jnp.zeros_like(values))


def inplane(fields, row_matrix, col_matrix):
    mixed = jnp.einsum("...xy,yv->...xv", fields, col_matrix, precision=highest)
    return jnp.einsum("...xy,xu->...uy", mixed, row_matrix, precision=highest)


def zwindow(fields, length, taps):
    summed = taps[0] * fields[..., 0:length, :, :]
    for offset in range(1, taps.shape[0]):
        summed = summed + taps[offset] * fields[..., offset : offset + length, :, :]
    return summed


def offset_weights(shift_axis, frac_axis):
    result = []
    for offset in range(-SHIFT, SHIFT + 2):
        lower = jnp.where(shift_axis == offset, 1.0 - frac_axis, 0.0)
        upper = jnp.where(shift_axis == offset - 1, frac_axis, 0.0)
        result.append(lower + upper)
    return result


def warp(padded_template, front, shift_one, frac_one):
    depth_len, row_len, col_len = frac_one.shape[1:]
    weights = frac_one.astype(jnp.float32)
    depth_w = offset_weights(shift_one[0], weights[0])
    row_w = offset_weights(shift_one[1], weights[1])
    col_w = offset_weights(shift_one[2], weights[2])
    summed = jnp.zeros(frac_one.shape[1:], jnp.float32)
    for kz in range(2 * SHIFT + 2):
        depth_start = front + kz - SHIFT
        plane_sum = jnp.zeros(frac_one.shape[1:], jnp.float32)
        for kr in range(2 * SHIFT + 2):
            line_sum = jnp.zeros(frac_one.shape[1:], jnp.float32)
            for kc in range(2 * SHIFT + 2):
                piece = padded_template[
                    depth_start : depth_start + depth_len, kr : kr + row_len, kc : kc + col_len
                ]
                line_sum = line_sum + col_w[kc] * piece
            plane_sum = plane_sum + row_w[kr] * line_sum
        summed = summed + depth_w[kz] * plane_sum
    return lax.optimization_barrier(summed.astype(jnp.bfloat16))


def correlation_force(warped_ext, subject_ext, length):
    row_count = warped_ext.shape[-2]
    col_count = warped_ext.shape[-1]
    stacked = jnp.stack(
        [
            warped_ext,
            subject_ext,
            warped_ext * warped_ext,
            subject_ext * subject_ext,
            warped_ext * subject_ext,
        ]
    )
    box_sums = inplane(stacked, band_matrix(row_count, WIN), band_matrix(col_count, WIN))
    window = float((2 * WIN + 1) ** 3)
    local_means = zwindow(box_sums, length, jnp.ones((2 * WIN + 1,), jnp.float32)) / window
    centre_warped = warped_ext[..., WIN : WIN + length, :, :]
    centre_subject = subject_ext[..., WIN : WIN + length, :, :]
    var_warped = local_means[2] - local_means[0] * local_means[0]
    var_subject = local_means[3] - local_means[1] * local_means[1]
    covariance = local_means[4] - local_means[0] * local_means[1]
    factor = (
        centre_subject
        - local_means[1]
        - covariance / (var_warped + epsilon) * (centre_warped - local_means[0])
    ) / jnp.sqrt(var_warped * var_subject + epsilon)
    grad_depth = 0.5 * (
        warped_ext[..., WIN + 1 : WIN + 1 + length, :, :]
        - warped_ext[..., WIN - 1 : WIN - 1 + length, :, :]
    )
    padded = jnp.pad(centre_warped, [(0, 0)] * (centre_warped.ndim - 2) + [(1, 1), (1, 1)])
    grad_rows = 0.5 * (padded[..., 2:, 1:-1] - padded[..., :-2, 1:-1])
    grad_cols = 0.5 * (padded[..., 1:-1, 2:] - padded[..., 1:-1, :-2])
    return jnp.stack([factor * grad_depth, factor * grad_rows, factor * grad_cols], axis=-4)


def smooth(force_ext, length):
    along = zwindow(force_ext, length, gauss_taps())
    return inplane(along, gauss_matrix(force_ext.shape[-2]), gauss_matrix(force_ext.shape[-1]))


def swap(block, axis, bit):
    count = lax.axis_size(axis)
    return lax.ppermute(block, axis, [(i, i ^ bit) for i in range(count)])


def bits_of(count):
    return [1 << place for place in range(count.bit_length() - 1)]


def gather_slab(block, axis):
    me = lax.axis_index(axis)
    for bit in bits_of(lax.axis_size(axis)):
        other = swap(block, axis, bit)
        upper = (me & bit) != 0
        block = jnp.concatenate(
            [jnp.where(upper, other, block), jnp.where(upper, block, other)], axis=0
        )
    return block


def scatter_sum(block, axis):
    me = lax.axis_index(axis)
    for bit in reversed(bits_of(lax.axis_size(axis))):
        half = block.shape[0] // 2
        upper = (me & bit) != 0
        low, high = block[:half], block[half:]
        block = jnp.where(upper, high, low) + swap(jnp.where(upper, low, high), axis, bit)
    return block


def per_device(template, subjects, shifts, fractions):
    slab_whole = gather_slab(template, "subj")
    slab_depth = slab_whole.shape[0]
    groups = lax.axis_size("gz")
    members = lax.axis_size("subj")
    extended = with_halo(slab_whole, (("gz", 0),), SHIFT + 1)
    padded_template = jnp.pad(
        extended.astype(jnp.float32), ((0, 0), (SHIFT, SHIFT + 1), (SHIFT, SHIFT + 1))
    )
    subject_count = subjects.shape[0]
    warped = jnp.stack([warp(padded_template, SHIFT + 1, shifts[0], fractions[0])])
    residual = jnp.sum(subjects.astype(jnp.float32) - warped.astype(jnp.float32), axis=0)
    paired = jnp.stack([warped, subjects])
    rimmed = with_halo(paired, (("gz", 2),), WIN + SMOOTH).astype(jnp.float32)
    force = correlation_force(rimmed[0], rimmed[1], slab_depth + 2 * SMOOTH)
    positions = (
        lax.axis_index("gz") * slab_depth
        - SMOOTH
        + jnp.arange(slab_depth + 2 * SMOOTH, dtype=jnp.int32)
    )
    inside = ((positions >= 0) & (positions < slab_depth * groups)).astype(jnp.float32)
    force_ext = force * inside[:, None, None]
    velocity_step = smooth(force_ext, slab_depth)
    own_rows = scatter_sum(residual, "subj")
    template_force = own_rows * (1.0 / math.sqrt(subject_count * members))
    return (velocity_step, template_force)


def solution(mesh):
    placed = (
        P(("gz", "subj"), None, None),
        P("subj", "gz", None, None),
        P("subj", None, "gz", None, None),
        P("subj", None, "gz", None, None),
    )
    return jax.shard_map(
        per_device,
        mesh=mesh,
        in_specs=placed,
        out_specs=(P("subj", None, "gz", None, None), P(("gz", "subj"), None, None)),
        check_vma=False,
    )
```

```python
import math

import jax
import jax.numpy as jnp
from jax import lax
from jax.experimental import pallas as pl
from jax.experimental.pallas import tpu as pltpu
from jax.sharding import PartitionSpec as P

SHIFT = 2
WIN = 4
SMOOTH = 4
EDGE = WIN + SMOOTH
HALO = EDGE + SHIFT + 1
TAPS = 2 * SHIFT + 2
sigma = 1.5
epsilon = 1e-05
f32 = jnp.float32
bf16 = jnp.bfloat16
VMEM_LIMIT = 48 * 1024 * 1024

raw = [math.exp(-k * k / (2 * sigma * sigma)) for k in range(SMOOTH + 1)]
norm = raw[0] + 2 * sum(raw[1:])
GAUSS = [value / norm for value in raw]


def swap(block, axis, bit):
    count = lax.axis_size(axis)
    return lax.ppermute(block, axis, [(i, i ^ bit) for i in range(count)])


def swap_near(block, axis):
    count = lax.axis_size(axis)
    pairs = [(i, i ^ 1) for i in range(count) if (i ^ 1) < count]
    return lax.ppermute(block, axis, pairs)


def swap_far(block, axis):
    count = lax.axis_size(axis)
    ups = [(i, i + 1) for i in range(1, count - 1, 2)]
    return lax.ppermute(block, axis, ups + [(target, source) for source, target in ups])


def bits_of(count):
    return [1 << place for place in range(count.bit_length() - 1)]


def mirrored(number, count):
    places = count.bit_length() - 1
    return sum(((number >> place) & 1) << (places - 1 - place) for place in range(places))


def scatter_sum(keep, send, axis, hold):
    for stage, bit in enumerate(bits_of(lax.axis_size(axis))):
        if stage:
            pairs = keep.reshape((-1, 2, share_of(keep, axis, stage)) + keep.shape[1:])
            keep, send = [pairs[:, part].reshape((-1,) + keep.shape[1:]) for part in (0, 1)]
        keep = hold(stage, keep + swap(send, axis, bit))
    return keep


def share_of(keep, axis, stage):
    return keep.shape[0] * (1 << stage) // lax.axis_size(axis)


def at_ends(axis, low, high):
    odd = lax.axis_index(axis) % 2 == 1
    return jnp.where(odd, low, high), jnp.where(odd, high, low)


def shift_matrix(offsets, cols):
    source = lax.broadcasted_iota(jnp.int32, (cols, cols), 0)
    target = lax.broadcasted_iota(jnp.int32, (cols, cols), 1)
    return jnp.concatenate(
        [(source == target + offset).astype(f32) for offset in offsets], axis=1
    ).astype(bf16)


def rows_at(value, index):
    return jnp.take_along_axis(value, index, axis=0, mode="promise_in_bounds")


def even_odd(base, frac):
    even = (base == -2.0) | (base == 0.0) | (base == 2.0)
    rest = 1.0 - frac
    return jnp.where(even, rest, frac), jnp.where(even, frac, rest)


def warp_slice(shifted, plane, sz, sr, sc, fz, fr, fc):
    rows = sz.shape[0]
    row = lax.broadcasted_iota(jnp.int32, sz.shape, 0).astype(f32) + sr
    top = rows - 1.0
    index0 = jnp.clip(row, 0.0, top).astype(jnp.int32)
    index1 = jnp.clip(row + 1.0, 0.0, top).astype(jnp.int32)
    weight0 = jnp.where((row >= 0.0) & (row <= top), 1.0 - fr, 0.0)
    weight1 = jnp.where((row >= -1.0) & (row <= top - 1.0), fr, 0.0)
    col_e, col_o = even_odd(sc, fc)
    dep_e, dep_o = even_odd(sz, fz)
    c1, c2, c3, c4 = [sc >= edge for edge in (-1.0, 0.0, 1.0, 2.0)]
    z1, z2, z3, z4 = [sz >= edge for edge in (-1.0, 0.0, 1.0, 2.0)]
    picks = {2: (c1, z1), 3: (c2, z2), 4: (c3, z3), 5: (c4, z4)}
    planes = [None, None]
    for kz in range(TAPS):
        corner = [[None, None], [None, None]]
        for kc in range(TAPS):
            value = shifted[kc, plane + kz]
            for b, index in ((0, index0), (1, index1)):
                taken = rows_at(value, index)
                if kc < 2:
                    corner[b][kc] = taken
                else:
                    corner[b][kc % 2] = jnp.where(picks[kc][0], taken, corner[b][kc % 2])
        flat = corner[0] + corner[1]
        if kz < 2:
            planes[kz] = flat
        else:
            mask = picks[kz][1]
            planes[kz % 2] = [jnp.where(mask, new, old) for new, old in zip(flat, planes[kz % 2])]
    parts = []
    for e0, o0, e1, o1 in planes:
        parts.append(
            weight0 * (col_e * e0 + col_o * o0) + weight1 * (col_e * e1 + col_o * o1)
        )
    summed = dep_e * parts[0] + dep_o * parts[1]
    return summed.astype(bf16).astype(f32)


def move_columns(slab, shifted, start, step):
    rows, cols = slab.shape[1:]
    offsets = [k - SHIFT for k in range(TAPS) if k != SHIFT]
    matrix = shift_matrix(offsets, cols)
    block = slab[start : start + step]
    shifted[SHIFT, start : start + step] = block
    moved = jnp.dot(
        block.reshape(step * rows, cols).astype(bf16), matrix, preferred_element_type=f32
    )
    for number, offset in enumerate(offsets):
        shifted[offset + SHIFT, start : start + step] = moved[
            :, number * cols : (number + 1) * cols
        ].reshape(step, rows, cols)


def vmem_specs(count):
    return [pl.BlockSpec(memory_space=pltpu.VMEM)] * count


SMEM_SPEC = pl.BlockSpec(memory_space=pltpu.SMEM)


def local_call(kernel, name, outs, inputs, scratch, flops, scalars=True):
    return pl.pallas_call(
        kernel,
        out_shape=[jax.ShapeDtypeStruct(shape, f32) for shape in outs],
        in_specs=([SMEM_SPEC] if scalars else []) + vmem_specs(inputs),
        out_specs=vmem_specs(len(outs)),
        scratch_shapes=[pltpu.VMEM(shape, f32) for shape in scratch],
        compiler_params=pltpu.CompilerParams(vmem_limit_bytes=VMEM_LIMIT),
        cost_estimate=pl.CostEstimate(flops=flops, bytes_accessed=8_000_000, transcendentals=0),
        name=name,
    )


def slice_fields(shifts, fractions, z):
    return [shifts[axis, z].astype(f32) for axis in range(3)] + [
        fractions[axis, z].astype(f32) for axis in range(3)
    ]


def build_inner_warp(depth, rows, cols, members):
    share = depth // members

    def kernel(place, pieces, shifts, fractions, warped, slab, shifted):
        me = place[1]
        for k in range(members):
            shard = me ^ mirrored(k, members)
            slab[pl.ds(shard * share, share)] = pieces[k * share : (k + 1) * share].astype(f32)
        for start in range(0, depth, depth // 2):
            move_columns(slab, shifted, start, depth // 2)

        def body(i, carry):
            z = i + EDGE
            warped[i] = warp_slice(shifted, z - SHIFT, *slice_fields(shifts, fractions, z))
            return carry

        lax.fori_loop(0, depth - 2 * EDGE, body, 0, unroll=2)

    return local_call(
        kernel, "inner_warp", [(depth - 2 * EDGE, rows, cols)], 3,
        [(depth, rows, cols), (TAPS, depth, rows, cols)], 1_000_000_000,
    )


def build_outer_warp(depth, rows, cols, members):
    share = depth // members
    ext = depth + 2 * EDGE
    planes = 2 * HALO

    def kernel(
        place, low_t, high_t, near_t, far_t, near_m, far_m, shifts, fractions, subjects, inner,
        warped, keep, send, slab, shifted,
    ):
        odd = place[0] % 2 == 1
        me = place[1]
        near, far = near_t[...].astype(f32), far_t[...].astype(f32)
        slab[0:HALO] = jnp.where(odd, near, far)
        slab[HALO:planes] = low_t[...].astype(f32)
        slab[planes : planes + HALO] = high_t[...].astype(f32)
        slab[planes + HALO : 2 * planes] = jnp.where(odd, far, near)
        move_columns(slab, shifted, 0, 2 * planes)
        warped[2 * EDGE : depth] = inner[...]

        def body(z, carry):
            def edge(low):
                fields = []
                for axis in range(6):
                    one, two = near_m[axis, z].astype(f32), far_m[axis, z].astype(f32)
                    fields.append(jnp.where(odd, one, two) if low else jnp.where(odd, two, one))
                return fields

            inside = depth - EDGE + z
            warped[z] = warp_slice(shifted, z + 1, *edge(True))
            warped[z + EDGE] = warp_slice(
                shifted, z + EDGE + 1, *slice_fields(shifts, fractions, z)
            )
            warped[z + depth] = warp_slice(
                shifted, planes + z + 1, *slice_fields(shifts, fractions, inside)
            )
            warped[z + depth + EDGE] = warp_slice(
                shifted, planes + z + EDGE + 1, *edge(False)
            )
            return carry

        lax.fori_loop(0, EDGE, body, 0)

        for k in range(members):
            shard = me ^ k
            target = send if k % 2 else keep
            start = shard * share
            target[(k // 2) * share : (k // 2 + 1) * share] = (
                subjects[pl.ds(start, share)].astype(f32) - warped[pl.ds(EDGE + start, share)]
            )

    half = (depth // 2, rows, cols)
    return local_call(
        kernel, "outer_warp", [(ext, rows, cols), half, half], 10,
        [(2 * planes, rows, cols), (TAPS, 2 * planes, rows, cols)], 600_000_000,
    )


def band(cols, radius):
    apart = jnp.abs(
        lax.broadcasted_iota(jnp.int32, (cols, cols), 0)
        - lax.broadcasted_iota(jnp.int32, (cols, cols), 1)
    )
    return (apart <= radius).astype(f32)


def column_difference(cols):
    apart = lax.broadcasted_iota(jnp.int32, (cols, cols), 0) - lax.broadcasted_iota(
        jnp.int32, (cols, cols), 1
    )
    return jnp.where(apart == 1, 0.5, jnp.where(apart == -1, -0.5, 0.0)).astype(f32)


def gauss_columns(cols):
    apart = jnp.abs(
        lax.broadcasted_iota(jnp.int32, (cols, cols), 0)
        - lax.broadcasted_iota(jnp.int32, (cols, cols), 1)
    )
    result = jnp.zeros((cols, cols), f32)
    for k, tap in enumerate(GAUSS):
        result = jnp.where(apart == k, f32(tap), result)
    return result


def split(value):
    high = value.astype(bf16)
    return high, (value - high.astype(f32)).astype(bf16)


def take_rows(value, index):
    return jnp.take_along_axis(value, index, axis=0, mode="promise_in_bounds")


def row_window(value, row):
    first = row < WIN
    half = value + take_rows(value, row ^ 1)
    half = half + take_rows(half, row ^ 2)
    outer = jnp.clip(jnp.where(first, row - 1, row + 1), 0, 2 * WIN - 1)
    outer_two = jnp.clip(jnp.where(first, row - 2, row + 2), 0, 2 * WIN - 1)
    reach = jnp.where(first, row, 2 * WIN - 1 - row)
    across = take_rows(value, row ^ WIN) + jnp.where(
        reach >= 1, take_rows(value, outer ^ WIN), 0.0
    )
    return half + across + jnp.where(reach >= 2, take_rows(across, outer_two), 0.0)


def z_windows(load, count):
    x = [load(k) for k in range(count + 2 * WIN)]
    two = [x[k] + x[k + 1] for k in range(count + 2 * WIN - 1)]
    four = [two[k] + two[k + 2] for k in range(count + 2 * WIN - 3)]
    return [four[k] + four[k + 4] + x[k + 8] for k in range(count)]


STEP = 8
CHUNK = 16
SCALE = 1.0 / float((2 * WIN + 1) ** 3)


def flat(value):
    return value.reshape(-1, value.shape[-1])


def square_columns(product, twice):
    pair = jnp.concatenate(split(product), axis=1)
    return jnp.dot(pair, twice, preferred_element_type=f32)


def build_image(depth, rows, cols):
    ext, mid = depth + 2 * EDGE, depth + 2 * SMOOTH

    def kernel(place, near_m, far_m, subjects, image, mean, variance, boxes):
        odd = place[0] % 2 == 1
        near, far = near_m[6].astype(f32), far_m[6].astype(f32)
        image[0:EDGE] = jnp.where(odd, near, far)
        image[EDGE : EDGE + depth] = subjects[...].astype(f32)
        image[EDGE + depth : ext] = jnp.where(odd, far, near)
        box = band(cols, WIN).astype(bf16)
        twice = jnp.concatenate([box, box], axis=0)

        def columns(i, carry):
            at = pl.ds(i * CHUNK, CHUNK)
            two = flat(image[at])
            results = [
                jnp.dot(two.astype(bf16), box, preferred_element_type=f32),
                square_columns(two * two, twice),
            ]
            for field, result in enumerate(results):
                boxes[field, at] = result.reshape(CHUNK, rows, cols)
            return carry

        lax.fori_loop(0, ext // CHUNK, columns, 0)
        row = lax.broadcasted_iota(jnp.int32, (rows, cols), 0)

        def local(i, carry):
            start = i * STEP
            one, two = [
                [row_window(v, row) * SCALE for v in z_windows(lambda k: boxes[f, start + k], STEP)]
                for f in range(2)
            ]
            for k in range(STEP):
                mean[start + k] = one[k]
                variance[start + k] = two[k] - one[k] * one[k]
            return carry

        lax.fori_loop(0, mid // STEP, local, 0)

    return local_call(
        kernel, "image",
        [(ext, rows, cols), (mid, rows, cols), (mid, rows, cols)], 3,
        [(2, ext, rows, cols)], 400_000_000,
    )


def build_boxes(depth, rows, cols):
    ext = depth + 2 * EDGE

    def kernel(warped, image, boxes, slope):
        box = band(cols, WIN)
        first = jnp.concatenate([box, column_difference(cols)], axis=1).astype(bf16)
        box = box.astype(bf16)
        twice = jnp.concatenate([box, box], axis=0)

        def columns(i, carry):
            at = pl.ds(i * CHUNK, CHUNK)
            one, two = flat(warped[at]), flat(image[at])
            both = jnp.dot(one.astype(bf16), first, preferred_element_type=f32)
            results = [both[:, :cols], square_columns(one * one, twice), square_columns(one * two, twice)]
            for field, result in enumerate(results):
                boxes[field, at] = result.reshape(CHUNK, rows, cols)
            slope[at] = both[:, cols:].reshape(CHUNK, rows, cols)
            return carry

        lax.fori_loop(0, ext // CHUNK, columns, 0)

    return local_call(
        kernel, "boxes", [(3, ext, rows, cols), (ext, rows, cols)], 2, [], 400_000_000, scalars=False
    )


def build_force(depth, rows, cols, groups):
    mid = depth + 2 * SMOOTH

    def kernel(place, warped, image, mean, variance, boxes, slope, force):
        row = lax.broadcasted_iota(jnp.int32, (rows, cols), 0)

        def local(i, carry):
            start = i * STEP
            means = [
                [row_window(v, row) * SCALE for v in z_windows(lambda k: boxes[f, start + k], STEP)]
                for f in range(3)
            ]
            for k in range(STEP):
                mi, mii, mij = [field[k] for field in means]
                mj, var_j = mean[start + k], variance[start + k]
                at = start + k + WIN
                centre = warped[at]
                var_i = mii - mi * mi
                cov = mij - mi * mj
                factor = (image[at] - mj - cov / (var_i + epsilon) * (centre - mi)) / jnp.sqrt(
                    var_i * var_j + epsilon
                )
                grad_z = 0.5 * (warped[at + 1] - warped[at - 1])
                below = jnp.where(row < rows - 1, pltpu.roll(centre, rows - 1, 0), 0.0)
                above = jnp.where(row > 0, pltpu.roll(centre, 1, 0), 0.0)
                force[0, start + k] = factor * grad_z
                force[1, start + k] = factor * (0.5 * (below - above))
                force[2, start + k] = factor * slope[at]
            return carry

        lax.fori_loop(0, mid // STEP, local, 0)

        @pl.when(place[0] == 0)
        def _():
            force[:, 0:SMOOTH] = jnp.zeros((3, SMOOTH, rows, cols), f32)

        @pl.when(place[0] == groups - 1)
        def _():
            force[:, mid - SMOOTH : mid] = jnp.zeros((3, SMOOTH, rows, cols), f32)

    return local_call(kernel, "force", [(3, mid, rows, cols)], 6, [], 600_000_000)


def build_smooth(depth, rows, cols):
    def kernel(force, velocity, padded):
        g_high, g_low = split(gauss_columns(cols))
        g_all = jnp.concatenate(
            [
                jnp.concatenate([g_high, g_low], axis=1),
                jnp.concatenate([g_high, jnp.zeros_like(g_low)], axis=1),
            ],
            axis=0,
        )
        padded[...] = jnp.zeros(padded.shape, f32)

        def finish(i, carry):
            start = i * STEP
            for axis in range(3):
                x = [force[axis, start + k] for k in range(STEP + 2 * SMOOTH)]
                for k in range(STEP):
                    value = GAUSS[0] * x[k + SMOOTH]
                    for d in range(1, SMOOTH + 1):
                        value = value + GAUSS[d] * (x[k + SMOOTH - d] + x[k + SMOOTH + d])
                    padded[axis, k, SMOOTH : SMOOTH + rows] = value
                mixed = GAUSS[0] * padded[axis, :, SMOOTH : SMOOTH + rows]
                for d in range(1, SMOOTH + 1):
                    mixed = mixed + GAUSS[d] * (
                        padded[axis, :, SMOOTH - d : SMOOTH - d + rows]
                        + padded[axis, :, SMOOTH + d : SMOOTH + d + rows]
                    )
                pair = jnp.concatenate(split(flat(mixed)), axis=1)
                done = jnp.dot(pair, g_all, preferred_element_type=f32)
                velocity[axis, pl.ds(start, STEP)] = (done[:, :cols] + done[:, cols:]).reshape(
                    STEP, rows, cols
                )
            return carry

        lax.fori_loop(0, depth // STEP, finish, 0)

    return local_call(
        kernel, "smooth", [(3, depth, rows, cols)], 1,
        [(3, STEP, rows + 2 * SMOOTH, cols)], 600_000_000, scalars=False,
    )


def per_device(template, subjects, shifts, fractions):
    groups = lax.axis_size("gz")
    members = lax.axis_size("subj")
    subject_count, depth, rows, cols = subjects.shape
    share = depth // members
    me = lax.axis_index("subj")
    place = jnp.stack([lax.axis_index("gz"), me]).astype(jnp.int32)

    pieces = template
    for bit in reversed(bits_of(members)):
        pieces = jnp.concatenate([pieces, swap(pieces, "subj", bit)], axis=0)

    def edge(start):
        parts = [shifts[0, :, start : start + EDGE].astype(bf16)]
        parts += [fractions[0, :, start : start + EDGE], subjects[:, start : start + EDGE]]
        return jnp.concatenate(parts, axis=0)

    to_near, to_far = at_ends("gz", edge(0), edge(depth - EDGE))
    near_m, far_m = swap_near(to_near, "gz"), swap_far(to_far, "gz")

    def shares(numbers):
        starts = [mirrored(me ^ number, members) * share for number in numbers]
        return jnp.concatenate(
            [lax.dynamic_slice_in_dim(pieces, start, share, 0) for start in starts], axis=0
        )

    reach = -(-HALO // share)
    low_t = shares(range(reach))[:HALO]
    high_t = shares(range(members - reach, members))[-HALO:]
    to_near, to_far = at_ends("gz", low_t, high_t)
    near_t, far_t = swap_near(to_near, "gz"), swap_far(to_far, "gz")

    image, mean, variance = build_image(depth, rows, cols)(place, near_m, far_m, subjects[0])
    (inner,) = build_inner_warp(depth, rows, cols, members)(place, pieces, shifts[0], fractions[0])
    warped, keep, send = build_outer_warp(depth, rows, cols, members)(
        place, low_t, high_t, near_t, far_t, near_m, far_m, shifts[0], fractions[0], subjects[0], inner
    )
    boxes, slope = build_boxes(depth, rows, cols)(warped, image)
    waiting = {"boxes": boxes}

    def hold(stage, value):
        if stage == 0:
            value, waiting["boxes"] = lax.optimization_barrier((value, waiting["boxes"]))
            (waiting["force"],) = build_force(depth, rows, cols, groups)(
                place, warped, image, mean, variance, waiting["boxes"], slope
            )
        if stage == 1:
            value, waiting["force"] = lax.optimization_barrier((value, waiting["force"]))
        return value

    own_rows = scatter_sum(keep, send, "subj", hold)
    (velocity,) = build_smooth(depth, rows, cols)(waiting["force"])
    template_force = own_rows * (1.0 / math.sqrt(subject_count * members))
    return (velocity[None], template_force)


def solution(mesh):
    placed = (
        P(("gz", "subj"), None, None),
        P("subj", "gz", None, None),
        P("subj", None, "gz", None, None),
        P("subj", None, "gz", None, None),
    )
    return jax.shard_map(
        per_device,
        mesh=mesh,
        in_specs=placed,
        out_specs=(P("subj", None, "gz", None, None), P(("gz", "subj"), None, None)),
        check_vma=False,
    )
```

```python
import math

import jax
import jax.numpy as jnp
from jax import lax
from jax.experimental import pallas as pl
from jax.experimental.pallas import tpu as pltpu
from jax.sharding import PartitionSpec as P

SHIFT = 2
WIN = 4
SMOOTH = 4
EDGE = WIN + SMOOTH
HALO = EDGE + SHIFT + 1
TAPS = 2 * SHIFT + 2
sigma = 1.5
epsilon = 1e-05
f32 = jnp.float32
bf16 = jnp.bfloat16
PEERS = 4
VMEM_LIMIT = 48 * 1024 * 1024

raw = [math.exp(-k * k / (2 * sigma * sigma)) for k in range(SMOOTH + 1)]
norm = raw[0] + 2 * sum(raw[1:])
GAUSS = [value / norm for value in raw]


def swap(block, axis, bit):
    count = lax.axis_size(axis)
    return lax.ppermute(block, axis, [(i, i ^ bit) for i in range(count)])


def swap_near(block, axis):
    count = lax.axis_size(axis)
    pairs = [(i, i ^ 1) for i in range(count) if (i ^ 1) < count]
    return lax.ppermute(block, axis, pairs)


def swap_far(block, axis):
    count = lax.axis_size(axis)
    assert count % 2 == 0
    return lax.ppermute(
        block, axis, [(i, (i + 1 if i % 2 else i - 1) % count) for i in range(count)]
    )


def has_far(group, groups):
    return (group != 0) & (group != groups - 1)


def bits_of(count):
    return [1 << place for place in range(count.bit_length() - 1)]


def mirrored(number, count):
    places = count.bit_length() - 1
    return sum(((number >> place) & 1) << (places - 1 - place) for place in range(places))


def at_ends(axis, low, high):
    odd = lax.axis_index(axis) % 2 == 1
    return jnp.where(odd, low, high), jnp.where(odd, high, low)


def shift_matrix(offsets, cols):
    source = lax.broadcasted_iota(jnp.int32, (cols, cols), 0)
    target = lax.broadcasted_iota(jnp.int32, (cols, cols), 1)
    return jnp.concatenate(
        [(source == target + offset).astype(f32) for offset in offsets], axis=1
    ).astype(bf16)


def rows_at(value, index):
    return jnp.take_along_axis(value, index, axis=0, mode="promise_in_bounds")


def even_odd(base, frac):
    even = (base == -2.0) | (base == 0.0) | (base == 2.0)
    rest = 1.0 - frac
    return jnp.where(even, rest, frac), jnp.where(even, frac, rest)


def warp_slice(shifted, plane, sz, sr, sc, fz, fr, fc):
    rows = sz.shape[0]
    row = lax.broadcasted_iota(jnp.int32, sz.shape, 0).astype(f32) + sr
    top = rows - 1.0
    index0 = jnp.clip(row, 0.0, top).astype(jnp.int32)
    index1 = jnp.clip(row + 1.0, 0.0, top).astype(jnp.int32)
    weight0 = jnp.where((row >= 0.0) & (row <= top), 1.0 - fr, 0.0)
    weight1 = jnp.where((row >= -1.0) & (row <= top - 1.0), fr, 0.0)
    col_e, col_o = even_odd(sc, fc)
    dep_e, dep_o = even_odd(sz, fz)
    c1, c2, c3, c4 = [sc >= edge for edge in (-1.0, 0.0, 1.0, 2.0)]
    z1, z2, z3, z4 = [sz >= edge for edge in (-1.0, 0.0, 1.0, 2.0)]
    picks = {2: (c1, z1), 3: (c2, z2), 4: (c3, z3), 5: (c4, z4)}
    planes = [None, None]
    for kz in range(TAPS):
        corner = [[None, None], [None, None]]
        for kc in range(TAPS):
            value = shifted[kc, plane + kz]
            for b, index in ((0, index0), (1, index1)):
                taken = rows_at(value, index)
                if kc < 2:
                    corner[b][kc] = taken
                else:
                    corner[b][kc % 2] = jnp.where(picks[kc][0], taken, corner[b][kc % 2])
        flat = corner[0] + corner[1]
        if kz < 2:
            planes[kz] = flat
        else:
            mask = picks[kz][1]
            planes[kz % 2] = [jnp.where(mask, new, old) for new, old in zip(flat, planes[kz % 2])]
    parts = []
    for e0, o0, e1, o1 in planes:
        parts.append(
            weight0 * (col_e * e0 + col_o * o0) + weight1 * (col_e * e1 + col_o * o1)
        )
    summed = dep_e * parts[0] + dep_o * parts[1]
    return summed.astype(bf16).astype(f32)


def move_columns(slab, shifted, start, step):
    rows, cols = slab.shape[1:]
    offsets = [k - SHIFT for k in range(TAPS) if k != SHIFT]
    matrix = shift_matrix(offsets, cols)
    block = slab[start : start + step]
    shifted[SHIFT, start : start + step] = block
    moved = jnp.dot(
        block.reshape(step * rows, cols).astype(bf16), matrix, preferred_element_type=f32
    )
    for number, offset in enumerate(offsets):
        shifted[offset + SHIFT, start : start + step] = moved[
            :, number * cols : (number + 1) * cols
        ].reshape(step, rows, cols)


def vmem_specs(count):
    return [pl.BlockSpec(memory_space=pltpu.VMEM)] * count


SMEM_SPEC = pl.BlockSpec(memory_space=pltpu.SMEM)


def local_call(kernel, name, outs, inputs, scratch, flops, scalars=True):
    return pl.pallas_call(
        kernel,
        out_shape=[jax.ShapeDtypeStruct(shape, f32) for shape in outs],
        in_specs=([SMEM_SPEC] if scalars else []) + vmem_specs(inputs),
        out_specs=vmem_specs(len(outs)),
        scratch_shapes=[pltpu.VMEM(shape, f32) for shape in scratch],
        compiler_params=pltpu.CompilerParams(vmem_limit_bytes=VMEM_LIMIT),
        cost_estimate=pl.CostEstimate(flops=flops, bytes_accessed=8_000_000, transcendentals=0),
        name=name,
    )


def slice_fields(shifts, fractions, z):
    return [shifts[axis, z].astype(f32) for axis in range(3)] + [
        fractions[axis, z].astype(f32) for axis in range(3)
    ]


def place_of_shard(me, shard, members):
    apart = me ^ shard
    quarter = members // PEERS
    return (apart & (PEERS - 1)) * quarter + mirrored(apart // PEERS, quarter)


def build_pack(depth, rows, cols, share):
    def kernel(place, template, shifts, fractions, subjects, near, far, mine, whole, parts, done):
        odd = place[0] % 2 == 1
        starts = (0, depth - EDGE)
        copies = [pltpu.make_async_copy(template, mine, done.at[6])]
        for end, start in enumerate(starts):
            at = pl.ds(start, EDGE)
            copies.append(pltpu.make_async_copy(shifts.at[:, at], whole.at[end], done.at[3 * end]))
            copies.append(
                pltpu.make_async_copy(fractions.at[:, at], parts.at[end, 0:3], done.at[3 * end + 1])
            )
            copies.append(
                pltpu.make_async_copy(subjects.at[at], parts.at[end, 3], done.at[3 * end + 2])
            )
        for copy in copies:
            copy.start()
        for copy in copies:
            copy.wait()
        for axis in range(7):
            if axis < 3:
                low, high = whole[0, axis].astype(f32), whole[1, axis].astype(f32)
            else:
                low, high = parts[0, axis - 3].astype(f32), parts[1, axis - 3].astype(f32)
            near[axis] = jnp.where(odd, low, high).astype(bf16)
            far[axis] = jnp.where(odd, high, low).astype(bf16)

    any_spec = pl.BlockSpec(memory_space=pl.ANY)
    message = jax.ShapeDtypeStruct((7, EDGE, rows, cols), bf16)
    return pl.pallas_call(
        kernel,
        out_shape=[message, message, jax.ShapeDtypeStruct((share, rows, cols), bf16)],
        in_specs=[SMEM_SPEC] + [any_spec] * 4,
        out_specs=vmem_specs(3),
        scratch_shapes=[
            pltpu.VMEM((2, 3, EDGE, rows, cols), jnp.int32),
            pltpu.VMEM((2, 4, EDGE, rows, cols), bf16),
            pltpu.SemaphoreType.DMA((7,)),
        ],
        compiler_params=pltpu.CompilerParams(vmem_limit_bytes=VMEM_LIMIT),
        cost_estimate=pl.CostEstimate(flops=1_000_000, bytes_accessed=2_000_000, transcendentals=0),
        name="pack",
    )


def build_inner_warp(depth, rows, cols, members):
    share = depth // members

    def kernel(place, pieces, shifts, fractions, warped, slab, shifted):
        me = place[1]
        quarter = members // PEERS
        for k in range(members):
            shard = me ^ (k // quarter + PEERS * mirrored(k % quarter, quarter))
            slab[pl.ds(shard * share, share)] = pieces[k * share : (k + 1) * share].astype(f32)
        for start in range(0, depth, depth // 2):
            move_columns(slab, shifted, start, depth // 2)

        def body(i, carry):
            z = i + EDGE
            warped[i] = warp_slice(shifted, z - SHIFT, *slice_fields(shifts, fractions, z))
            return carry

        lax.fori_loop(0, depth - 2 * EDGE, body, 0, unroll=2)

    return local_call(
        kernel, "inner_warp", [(depth - 2 * EDGE, rows, cols)], 3,
        [(depth, rows, cols), (TAPS, depth, rows, cols)], 1_000_000_000,
    )


def build_outer_warp(depth, rows, cols, members, groups):
    share = depth // members
    ext = depth + 2 * EDGE
    planes = 2 * HALO

    def kernel(
        place, low_t, high_t, near_t, far_t, near_m, far_m, shifts, fractions, subjects, inner,
        warped, keep, send1, send2, send3, slab, shifted,
    ):
        odd = place[0] % 2 == 1
        me = place[1]
        inside = has_far(place[0], groups)
        near, far = near_t[...].astype(f32), jnp.where(inside, far_t[...].astype(f32), 0.0)
        slab[0:HALO] = jnp.where(odd, near, far)
        slab[HALO:planes] = low_t[...].astype(f32)
        slab[planes : planes + HALO] = high_t[...].astype(f32)
        slab[planes + HALO : 2 * planes] = jnp.where(odd, far, near)
        move_columns(slab, shifted, 0, 2 * planes)
        warped[2 * EDGE : depth] = inner[...]

        def body(z, carry):
            def edge(low):
                fields = []
                for axis in range(6):
                    one = near_m[axis, z].astype(f32)
                    two = jnp.where(inside, far_m[axis, z].astype(f32), 0.0)
                    fields.append(jnp.where(odd, one, two) if low else jnp.where(odd, two, one))
                return fields

            last = depth - EDGE + z
            warped[z] = warp_slice(shifted, z + 1, *edge(True))
            warped[z + EDGE] = warp_slice(
                shifted, z + EDGE + 1, *slice_fields(shifts, fractions, z)
            )
            warped[z + depth] = warp_slice(
                shifted, planes + z + 1, *slice_fields(shifts, fractions, last)
            )
            warped[z + depth + EDGE] = warp_slice(
                shifted, planes + z + EDGE + 1, *edge(False)
            )
            return carry

        lax.fori_loop(0, EDGE, body, 0)

        for k in range(members):
            shard = me ^ k
            target = (keep, send1, send2, send3)[k % PEERS]
            start = shard * share
            target[(k // PEERS) * share : (k // PEERS + 1) * share] = (
                subjects[pl.ds(start, share)].astype(f32) - warped[pl.ds(EDGE + start, share)]
            )

    part = (depth // PEERS, rows, cols)
    return local_call(
        kernel, "outer_warp", [(ext, rows, cols)] + [part] * PEERS, 10,
        [(2 * planes, rows, cols), (TAPS, 2 * planes, rows, cols)], 600_000_000,
    )


def band(cols, radius):
    apart = jnp.abs(
        lax.broadcasted_iota(jnp.int32, (cols, cols), 0)
        - lax.broadcasted_iota(jnp.int32, (cols, cols), 1)
    )
    return (apart <= radius).astype(f32)


def column_difference(cols):
    apart = lax.broadcasted_iota(jnp.int32, (cols, cols), 0) - lax.broadcasted_iota(
        jnp.int32, (cols, cols), 1
    )
    return jnp.where(apart == 1, 0.5, jnp.where(apart == -1, -0.5, 0.0)).astype(f32)


def gauss_columns(cols):
    apart = jnp.abs(
        lax.broadcasted_iota(jnp.int32, (cols, cols), 0)
        - lax.broadcasted_iota(jnp.int32, (cols, cols), 1)
    )
    result = jnp.zeros((cols, cols), f32)
    for k, tap in enumerate(GAUSS):
        result = jnp.where(apart == k, f32(tap), result)
    return result


def split(value):
    high = value.astype(bf16)
    return high, (value - high.astype(f32)).astype(bf16)


def take_rows(value, index):
    return jnp.take_along_axis(value, index, axis=0, mode="promise_in_bounds")


def row_window(value, row):
    first = row < WIN
    half = value + take_rows(value, row ^ 1)
    half = half + take_rows(half, row ^ 2)
    outer = jnp.clip(jnp.where(first, row - 1, row + 1), 0, 2 * WIN - 1)
    outer_two = jnp.clip(jnp.where(first, row - 2, row + 2), 0, 2 * WIN - 1)
    reach = jnp.where(first, row, 2 * WIN - 1 - row)
    across = take_rows(value, row ^ WIN) + jnp.where(
        reach >= 1, take_rows(value, outer ^ WIN), 0.0
    )
    return half + across + jnp.where(reach >= 2, take_rows(across, outer_two), 0.0)


def z_windows(load, count):
    x = [load(k) for k in range(count + 2 * WIN)]
    two = [x[k] + x[k + 1] for k in range(count + 2 * WIN - 1)]
    four = [two[k] + two[k + 2] for k in range(count + 2 * WIN - 3)]
    return [four[k] + four[k + 4] + x[k + 8] for k in range(count)]


STEP = 8
CHUNK = 16
SCALE = 1.0 / float((2 * WIN + 1) ** 3)


def flat(value):
    return value.reshape(-1, value.shape[-1])


def square_columns(product, twice):
    pair = jnp.concatenate(split(product), axis=1)
    return jnp.dot(pair, twice, preferred_element_type=f32)


def build_image(depth, rows, cols, groups):
    ext, mid = depth + 2 * EDGE, depth + 2 * SMOOTH

    def kernel(place, near_m, far_m, subjects, image, mean, variance, boxes):
        odd = place[0] % 2 == 1
        near = near_m[6].astype(f32)
        far = jnp.where(has_far(place[0], groups), far_m[6].astype(f32), 0.0)
        image[0:EDGE] = jnp.where(odd, near, far)
        image[EDGE : EDGE + depth] = subjects[...].astype(f32)
        image[EDGE + depth : ext] = jnp.where(odd, far, near)
        box = band(cols, WIN).astype(bf16)
        twice = jnp.concatenate([box, box], axis=0)

        def columns(i, carry):
            at = pl.ds(i * CHUNK, CHUNK)
            two = flat(image[at])
            results = [
                jnp.dot(two.astype(bf16), box, preferred_element_type=f32),
                square_columns(two * two, twice),
            ]
            for field, result in enumerate(results):
                boxes[field, at] = result.reshape(CHUNK, rows, cols)
            return carry

        lax.fori_loop(0, ext // CHUNK, columns, 0)
        row = lax.broadcasted_iota(jnp.int32, (rows, cols), 0)

        def local(i, carry):
            start = i * STEP
            one, two = [
                [row_window(v, row) * SCALE for v in z_windows(lambda k: boxes[f, start + k], STEP)]
                for f in range(2)
            ]
            for k in range(STEP):
                mean[start + k] = one[k]
                variance[start + k] = two[k] - one[k] * one[k]
            return carry

        lax.fori_loop(0, mid // STEP, local, 0)

    return local_call(
        kernel, "image",
        [(ext, rows, cols), (mid, rows, cols), (mid, rows, cols)], 3,
        [(2, ext, rows, cols)], 400_000_000,
    )


def build_force(depth, rows, cols, groups):
    ext, mid = depth + 2 * EDGE, depth + 2 * SMOOTH

    def kernel(place, warped, image, mean, variance, force, boxes, slope):
        box = band(cols, WIN)
        first = jnp.concatenate([box, column_difference(cols)], axis=1).astype(bf16)
        box = box.astype(bf16)
        twice = jnp.concatenate([box, box], axis=0)

        def columns(i, carry):
            at = pl.ds(i * CHUNK, CHUNK)
            one, two = flat(warped[at]), flat(image[at])
            both = jnp.dot(one.astype(bf16), first, preferred_element_type=f32)
            results = [both[:, :cols], square_columns(one * one, twice), square_columns(one * two, twice)]
            for field, result in enumerate(results):
                boxes[field, at] = result.reshape(CHUNK, rows, cols)
            slope[at] = both[:, cols:].reshape(CHUNK, rows, cols)
            return carry

        lax.fori_loop(0, ext // CHUNK, columns, 0)
        row = lax.broadcasted_iota(jnp.int32, (rows, cols), 0)

        def local(i, carry):
            start = i * STEP
            means = [
                [row_window(v, row) * SCALE for v in z_windows(lambda k: boxes[f, start + k], STEP)]
                for f in range(3)
            ]
            for k in range(STEP):
                mi, mii, mij = [field[k] for field in means]
                mj, var_j = mean[start + k], variance[start + k]
                at = start + k + WIN
                centre = warped[at]
                var_i = mii - mi * mi
                cov = mij - mi * mj
                factor = (image[at] - mj - cov / (var_i + epsilon) * (centre - mi)) / jnp.sqrt(
                    var_i * var_j + epsilon
                )
                grad_z = 0.5 * (warped[at + 1] - warped[at - 1])
                below = jnp.where(row < rows - 1, pltpu.roll(centre, rows - 1, 0), 0.0)
                above = jnp.where(row > 0, pltpu.roll(centre, 1, 0), 0.0)
                force[0, start + k] = factor * grad_z
                force[1, start + k] = factor * (0.5 * (below - above))
                force[2, start + k] = factor * slope[at]
            return carry

        lax.fori_loop(0, mid // STEP, local, 0)

        @pl.when(place[0] == 0)
        def _():
            force[:, 0:SMOOTH] = jnp.zeros((3, SMOOTH, rows, cols), f32)

        @pl.when(place[0] == groups - 1)
        def _():
            force[:, mid - SMOOTH : mid] = jnp.zeros((3, SMOOTH, rows, cols), f32)

    return local_call(
        kernel, "force", [(3, mid, rows, cols)], 4,
        [(3, ext, rows, cols), (ext, rows, cols)], 1_000_000_000,
    )


def build_smooth(depth, rows, cols):
    def kernel(force, velocity, padded):
        g_high, g_low = split(gauss_columns(cols))
        g_all = jnp.concatenate(
            [
                jnp.concatenate([g_high, g_low], axis=1),
                jnp.concatenate([g_high, jnp.zeros_like(g_low)], axis=1),
            ],
            axis=0,
        )
        padded[...] = jnp.zeros(padded.shape, f32)

        def finish(i, carry):
            start = i * STEP
            for axis in range(3):
                x = [force[axis, start + k] for k in range(STEP + 2 * SMOOTH)]
                for k in range(STEP):
                    value = GAUSS[0] * x[k + SMOOTH]
                    for d in range(1, SMOOTH + 1):
                        value = value + GAUSS[d] * (x[k + SMOOTH - d] + x[k + SMOOTH + d])
                    padded[axis, k, SMOOTH : SMOOTH + rows] = value
                mixed = GAUSS[0] * padded[axis, :, SMOOTH : SMOOTH + rows]
                for d in range(1, SMOOTH + 1):
                    mixed = mixed + GAUSS[d] * (
                        padded[axis, :, SMOOTH - d : SMOOTH - d + rows]
                        + padded[axis, :, SMOOTH + d : SMOOTH + d + rows]
                    )
                pair = jnp.concatenate(split(flat(mixed)), axis=1)
                done = jnp.dot(pair, g_all, preferred_element_type=f32)
                velocity[axis, pl.ds(start, STEP)] = (done[:, :cols] + done[:, cols:]).reshape(
                    STEP, rows, cols
                )
            return carry

        lax.fori_loop(0, depth // STEP, finish, 0)

    return local_call(
        kernel, "smooth", [(3, depth, rows, cols)], 1,
        [(3, STEP, rows + 2 * SMOOTH, cols)], 600_000_000, scalars=False,
    )


def per_device(template, subjects, shifts, fractions):
    groups = lax.axis_size("gz")
    members = lax.axis_size("subj")
    subject_count, depth, rows, cols = subjects.shape
    share = depth // members
    reach = -(-HALO // share)
    me = lax.axis_index("subj")
    place = jnp.stack([lax.axis_index("gz"), me]).astype(jnp.int32)
    bits = bits_of(members)[2:]
    subject, shift, fraction = subjects[0], shifts[0], fractions[0]

    arrived = swap(template, "subj", bits[-1])
    to_near, to_far, mine = build_pack(depth, rows, cols, share)(
        place, template, shift, fraction, subject
    )
    pieces = jnp.concatenate([mine, arrived], axis=0)
    near_m, far_m = swap_near(to_near, "gz"), swap_far(to_far, "gz")
    pieces, subject = lax.optimization_barrier((pieces, subject))
    for bit in bits[-2::-1]:
        pieces = jnp.concatenate([pieces, swap(pieces, "subj", bit)], axis=0)
    pieces = jnp.concatenate(
        [pieces] + [swap(pieces, "subj", k) for k in range(1, PEERS)], axis=0
    )

    def shares(numbers):
        starts = [place_of_shard(me, number, members) * share for number in numbers]
        return jnp.concatenate(
            [lax.dynamic_slice_in_dim(pieces, start, share, 0) for start in starts], axis=0
        )

    low_t = shares(range(reach))[:HALO]
    high_t = shares(range(members - reach, members))[-HALO:]
    to_near, to_far = at_ends("gz", low_t, high_t)
    near_t, far_t = swap_near(to_near, "gz"), swap_far(to_far, "gz")

    (inner,) = build_inner_warp(depth, rows, cols, members)(place, pieces, shift, fraction)
    warped, keep, *sends = build_outer_warp(depth, rows, cols, members, groups)(
        place, low_t, high_t, near_t, far_t, near_m, far_m, shift, fraction, subject, inner
    )

    parts = [swap(send, "subj", k) for k, send in zip(range(1, PEERS), sends)]
    near_m, far_m, subject, warped = lax.optimization_barrier((near_m, far_m, subject, warped))
    image, mean, variance = build_image(depth, rows, cols, groups)(place, near_m, far_m, subject)
    (force,) = build_force(depth, rows, cols, groups)(place, warped, image, mean, variance)
    *parts, force = lax.optimization_barrier((*parts, force))
    keep = keep + parts[0] + parts[1] + parts[2]
    for bit in bits:
        pairs = keep.reshape((-1, 2, share) + keep.shape[1:])
        keep, send = [pairs[:, part].reshape((-1,) + keep.shape[1:]) for part in (0, 1)]
        keep = keep + swap(send, "subj", bit)
    (velocity,) = build_smooth(depth, rows, cols)(force)
    template_force = keep * (1.0 / math.sqrt(subject_count * members))
    return (velocity[None], template_force)


def solution(mesh):
    placed = (
        P(("gz", "subj"), None, None),
        P("subj", "gz", None, None),
        P("subj", None, "gz", None, None),
        P("subj", None, "gz", None, None),
    )
    return jax.shard_map(
        per_device,
        mesh=mesh,
        in_specs=placed,
        out_specs=(P("subj", None, "gz", None, None), P(("gz", "subj"), None, None)),
        check_vma=False,
    )
```

```python
import math

import jax
import jax.numpy as jnp
from jax import lax
from jax.experimental import pallas as pl
from jax.experimental.pallas import tpu as pltpu
from jax.sharding import PartitionSpec as P

SHIFT = 2
WIN = 4
SMOOTH = 4
EDGE = WIN + SMOOTH
HALO = EDGE + SHIFT + 1
TAPS = 2 * SHIFT + 2
sigma = 1.5
epsilon = 1e-05
f32 = jnp.float32
bf16 = jnp.bfloat16
PEERS = 4
VMEM_LIMIT = 48 * 1024 * 1024

raw = [math.exp(-k * k / (2 * sigma * sigma)) for k in range(SMOOTH + 1)]
norm = raw[0] + 2 * sum(raw[1:])
GAUSS = [value / norm for value in raw]


def swap(block, axis, bit):
    count = lax.axis_size(axis)
    return lax.ppermute(block, axis, [(i, i ^ bit) for i in range(count)])


def swap_near(block, axis):
    count = lax.axis_size(axis)
    pairs = [(i, i ^ 1) for i in range(count) if (i ^ 1) < count]
    return lax.ppermute(block, axis, pairs)


def swap_far(block, axis):
    count = lax.axis_size(axis)
    assert count % 2 == 0
    return lax.ppermute(
        block, axis, [(i, (i + 1 if i % 2 else i - 1) % count) for i in range(count)]
    )


def has_far(group, groups):
    return (group != 0) & (group != groups - 1)


def bits_of(count):
    return [1 << place for place in range(count.bit_length() - 1)]


def mirrored(number, count):
    places = count.bit_length() - 1
    return sum(((number >> place) & 1) << (places - 1 - place) for place in range(places))


def at_ends(axis, low, high):
    odd = lax.axis_index(axis) % 2 == 1
    return jnp.where(odd, low, high), jnp.where(odd, high, low)


def shift_matrix(offsets, cols):
    source = lax.broadcasted_iota(jnp.int32, (cols, cols), 0)
    target = lax.broadcasted_iota(jnp.int32, (cols, cols), 1)
    return jnp.concatenate(
        [(source == target + offset).astype(f32) for offset in offsets], axis=1
    ).astype(bf16)


def rows_at(value, index):
    return jnp.take_along_axis(value, index, axis=0, mode="promise_in_bounds")


def even_odd(base, frac):
    even = (base == -2.0) | (base == 0.0) | (base == 2.0)
    rest = 1.0 - frac
    return jnp.where(even, rest, frac), jnp.where(even, frac, rest)


def warp_slice(shifted, plane, sz, sr, sc, fz, fr, fc):
    rows = sz.shape[0]
    row = lax.broadcasted_iota(jnp.int32, sz.shape, 0).astype(f32) + sr
    top = rows - 1.0
    index0 = jnp.clip(row, 0.0, top).astype(jnp.int32)
    index1 = jnp.clip(row + 1.0, 0.0, top).astype(jnp.int32)
    weight0 = jnp.where((row >= 0.0) & (row <= top), 1.0 - fr, 0.0)
    weight1 = jnp.where((row >= -1.0) & (row <= top - 1.0), fr, 0.0)
    col_e, col_o = even_odd(sc, fc)
    dep_e, dep_o = even_odd(sz, fz)
    c1, c2, c3, c4 = [sc >= edge for edge in (-1.0, 0.0, 1.0, 2.0)]
    z1, z2, z3, z4 = [sz >= edge for edge in (-1.0, 0.0, 1.0, 2.0)]
    picks = {2: (c1, z1), 3: (c2, z2), 4: (c3, z3), 5: (c4, z4)}
    planes = [None, None]
    for kz in range(TAPS):
        corner = [[None, None], [None, None]]
        for kc in range(TAPS):
            value = shifted[kc, plane + kz]
            for b, index in ((0, index0), (1, index1)):
                taken = rows_at(value, index)
                if kc < 2:
                    corner[b][kc] = taken
                else:
                    corner[b][kc % 2] = jnp.where(picks[kc][0], taken, corner[b][kc % 2])
        flat = corner[0] + corner[1]
        if kz < 2:
            planes[kz] = flat
        else:
            mask = picks[kz][1]
            planes[kz % 2] = [jnp.where(mask, new, old) for new, old in zip(flat, planes[kz % 2])]
    parts = []
    for e0, o0, e1, o1 in planes:
        parts.append(
            weight0 * (col_e * e0 + col_o * o0) + weight1 * (col_e * e1 + col_o * o1)
        )
    summed = dep_e * parts[0] + dep_o * parts[1]
    return summed.astype(bf16).astype(f32)


def move_columns(slab, shifted, start, step):
    rows, cols = slab.shape[1:]
    offsets = [k - SHIFT for k in range(TAPS) if k != SHIFT]
    matrix = shift_matrix(offsets, cols)
    block = slab[start : start + step]
    shifted[SHIFT, start : start + step] = block
    moved = jnp.dot(
        block.reshape(step * rows, cols).astype(bf16), matrix, preferred_element_type=f32
    )
    for number, offset in enumerate(offsets):
        shifted[offset + SHIFT, start : start + step] = moved[
            :, number * cols : (number + 1) * cols
        ].reshape(step, rows, cols)


def vmem_specs(count):
    return [pl.BlockSpec(memory_space=pltpu.VMEM)] * count


def local_call(kernel, name, outs, inputs, scratch, flops):
    return pl.pallas_call(
        kernel,
        out_shape=[jax.ShapeDtypeStruct(shape, f32) for shape in outs],
        in_specs=vmem_specs(inputs),
        out_specs=vmem_specs(len(outs)),
        scratch_shapes=[pltpu.VMEM(shape, f32) for shape in scratch],
        compiler_params=pltpu.CompilerParams(vmem_limit_bytes=VMEM_LIMIT),
        cost_estimate=pl.CostEstimate(flops=flops, bytes_accessed=8_000_000, transcendentals=0),
        name=name,
    )


def slice_fields(shifts, fractions, z):
    return [shifts[axis, z].astype(f32) for axis in range(3)] + [
        fractions[axis, z].astype(f32) for axis in range(3)
    ]


def place_of_shard(me, shard, members):
    apart = me ^ shard
    quarter = members // PEERS
    return (apart & (PEERS - 1)) * quarter + mirrored(apart // PEERS, quarter)


def build_pack(depth, rows, cols, share):
    def kernel(template, shifts, fractions, subjects, near, far, mine, whole, parts, done):
        odd = lax.axis_index("gz") % 2 == 1
        starts = (0, depth - EDGE)
        copies = [pltpu.make_async_copy(template, mine, done.at[6])]
        for end, start in enumerate(starts):
            at = pl.ds(start, EDGE)
            copies.append(pltpu.make_async_copy(shifts.at[:, at], whole.at[end], done.at[3 * end]))
            copies.append(
                pltpu.make_async_copy(fractions.at[:, at], parts.at[end, 0:3], done.at[3 * end + 1])
            )
            copies.append(
                pltpu.make_async_copy(subjects.at[at], parts.at[end, 3], done.at[3 * end + 2])
            )
        for copy in copies:
            copy.start()
        for copy in copies:
            copy.wait()
        for axis in range(7):
            if axis < 3:
                low, high = whole[0, axis].astype(f32), whole[1, axis].astype(f32)
            else:
                low, high = parts[0, axis - 3].astype(f32), parts[1, axis - 3].astype(f32)
            near[axis] = jnp.where(odd, low, high).astype(bf16)
            far[axis] = jnp.where(odd, high, low).astype(bf16)

    any_spec = pl.BlockSpec(memory_space=pl.ANY)
    message = jax.ShapeDtypeStruct((7, EDGE, rows, cols), bf16)
    return pl.pallas_call(
        kernel,
        out_shape=[message, message, jax.ShapeDtypeStruct((share, rows, cols), bf16)],
        in_specs=[any_spec] * 4,
        out_specs=vmem_specs(3),
        scratch_shapes=[
            pltpu.VMEM((2, 3, EDGE, rows, cols), jnp.int32),
            pltpu.VMEM((2, 4, EDGE, rows, cols), bf16),
            pltpu.SemaphoreType.DMA((7,)),
        ],
        compiler_params=pltpu.CompilerParams(vmem_limit_bytes=VMEM_LIMIT),
        cost_estimate=pl.CostEstimate(flops=1_000_000, bytes_accessed=2_000_000, transcendentals=0),
        name="pack",
    )


def build_inner_warp(depth, rows, cols, members):
    share = depth // members

    def kernel(pieces, shifts, fractions, warped, slab, shifted):
        me = lax.axis_index("subj")
        quarter = members // PEERS
        for k in range(members):
            shard = me ^ (k // quarter + PEERS * mirrored(k % quarter, quarter))
            slab[pl.ds(shard * share, share)] = pieces[k * share : (k + 1) * share].astype(f32)
        for start in range(0, depth, depth // 2):
            move_columns(slab, shifted, start, depth // 2)

        def body(i, carry):
            z = i + EDGE
            warped[i] = warp_slice(shifted, z - SHIFT, *slice_fields(shifts, fractions, z))
            return carry

        lax.fori_loop(0, depth - 2 * EDGE, body, 0, unroll=2)

    return local_call(
        kernel, "inner_warp", [(depth - 2 * EDGE, rows, cols)], 3,
        [(depth, rows, cols), (TAPS, depth, rows, cols)], 1_000_000_000,
    )


def build_outer_warp(depth, rows, cols, members, groups):
    share = depth // members
    ext = depth + 2 * EDGE
    planes = 2 * HALO

    def kernel(
        low_t, high_t, near_t, far_t, near_m, far_m, shifts, fractions, subjects, inner,
        warped, keep, send1, send2, send3, slab, shifted,
    ):
        odd = lax.axis_index("gz") % 2 == 1
        me = lax.axis_index("subj")
        inside = has_far(lax.axis_index("gz"), groups)
        near, far = near_t[...].astype(f32), jnp.where(inside, far_t[...].astype(f32), 0.0)
        slab[0:HALO] = jnp.where(odd, near, far)
        slab[HALO:planes] = low_t[...].astype(f32)
        slab[planes : planes + HALO] = high_t[...].astype(f32)
        slab[planes + HALO : 2 * planes] = jnp.where(odd, far, near)
        move_columns(slab, shifted, 0, 2 * planes)
        warped[2 * EDGE : depth] = inner[...]

        def body(z, carry):
            def edge(low):
                fields = []
                for axis in range(6):
                    one = near_m[axis, z].astype(f32)
                    two = jnp.where(inside, far_m[axis, z].astype(f32), 0.0)
                    fields.append(jnp.where(odd, one, two) if low else jnp.where(odd, two, one))
                return fields

            last = depth - EDGE + z
            warped[z] = warp_slice(shifted, z + 1, *edge(True))
            warped[z + EDGE] = warp_slice(
                shifted, z + EDGE + 1, *slice_fields(shifts, fractions, z)
            )
            warped[z + depth] = warp_slice(
                shifted, planes + z + 1, *slice_fields(shifts, fractions, last)
            )
            warped[z + depth + EDGE] = warp_slice(
                shifted, planes + z + EDGE + 1, *edge(False)
            )
            return carry

        lax.fori_loop(0, EDGE, body, 0)

        for k in range(members):
            shard = me ^ k
            target = (keep, send1, send2, send3)[k % PEERS]
            start = shard * share
            target[(k // PEERS) * share : (k // PEERS + 1) * share] = (
                subjects[pl.ds(start, share)].astype(f32) - warped[pl.ds(EDGE + start, share)]
            )

    part = (depth // PEERS, rows, cols)
    return local_call(
        kernel, "outer_warp", [(ext, rows, cols)] + [part] * PEERS, 10,
        [(2 * planes, rows, cols), (TAPS, 2 * planes, rows, cols)], 600_000_000,
    )


def band(cols, radius):
    apart = jnp.abs(
        lax.broadcasted_iota(jnp.int32, (cols, cols), 0)
        - lax.broadcasted_iota(jnp.int32, (cols, cols), 1)
    )
    return (apart <= radius).astype(f32)


def column_difference(cols):
    apart = lax.broadcasted_iota(jnp.int32, (cols, cols), 0) - lax.broadcasted_iota(
        jnp.int32, (cols, cols), 1
    )
    return jnp.where(apart == 1, 0.5, jnp.where(apart == -1, -0.5, 0.0)).astype(f32)


def gauss_columns(cols):
    apart = jnp.abs(
        lax.broadcasted_iota(jnp.int32, (cols, cols), 0)
        - lax.broadcasted_iota(jnp.int32, (cols, cols), 1)
    )
    result = jnp.zeros((cols, cols), f32)
    for k, tap in enumerate(GAUSS):
        result = jnp.where(apart == k, f32(tap), result)
    return result


def split(value):
    high = value.astype(bf16)
    return high, (value - high.astype(f32)).astype(bf16)


def take_rows(value, index):
    return jnp.take_along_axis(value, index, axis=0, mode="promise_in_bounds")


def row_window(value, row):
    first = row < WIN
    half = value + take_rows(value, row ^ 1)
    half = half + take_rows(half, row ^ 2)
    outer = jnp.clip(jnp.where(first, row - 1, row + 1), 0, 2 * WIN - 1)
    outer_two = jnp.clip(jnp.where(first, row - 2, row + 2), 0, 2 * WIN - 1)
    reach = jnp.where(first, row, 2 * WIN - 1 - row)
    across = take_rows(value, row ^ WIN) + jnp.where(
        reach >= 1, take_rows(value, outer ^ WIN), 0.0
    )
    return half + across + jnp.where(reach >= 2, take_rows(across, outer_two), 0.0)


def z_windows(load, count):
    x = [load(k) for k in range(count + 2 * WIN)]
    two = [x[k] + x[k + 1] for k in range(count + 2 * WIN - 1)]
    four = [two[k] + two[k + 2] for k in range(count + 2 * WIN - 3)]
    return [four[k] + four[k + 4] + x[k + 8] for k in range(count)]


STEP = 8
CHUNK = 16
SCALE = 1.0 / float((2 * WIN + 1) ** 3)


def flat(value):
    return value.reshape(-1, value.shape[-1])


def square_columns(product, twice):
    pair = jnp.concatenate(split(product), axis=1)
    return jnp.dot(pair, twice, preferred_element_type=f32)


def build_image(depth, rows, cols, groups):
    ext, mid = depth + 2 * EDGE, depth + 2 * SMOOTH

    def kernel(near_m, far_m, subjects, image, mean, variance, boxes):
        odd = lax.axis_index("gz") % 2 == 1
        near = near_m[6].astype(f32)
        far = jnp.where(has_far(lax.axis_index("gz"), groups), far_m[6].astype(f32), 0.0)
        image[0:EDGE] = jnp.where(odd, near, far)
        image[EDGE : EDGE + depth] = subjects[...].astype(f32)
        image[EDGE + depth : ext] = jnp.where(odd, far, near)
        box = band(cols, WIN).astype(bf16)
        twice = jnp.concatenate([box, box], axis=0)

        def columns(i, carry):
            at = pl.ds(i * CHUNK, CHUNK)
            two = flat(image[at])
            results = [
                jnp.dot(two.astype(bf16), box, preferred_element_type=f32),
                square_columns(two * two, twice),
            ]
            for field, result in enumerate(results):
                boxes[field, at] = result.reshape(CHUNK, rows, cols)
            return carry

        lax.fori_loop(0, ext // CHUNK, columns, 0)
        row = lax.broadcasted_iota(jnp.int32, (rows, cols), 0)

        def local(i, carry):
            start = i * STEP
            one, two = [
                [row_window(v, row) * SCALE for v in z_windows(lambda k: boxes[f, start + k], STEP)]
                for f in range(2)
            ]
            for k in range(STEP):
                mean[start + k] = one[k]
                variance[start + k] = two[k] - one[k] * one[k]
            return carry

        lax.fori_loop(0, mid // STEP, local, 0)

    return local_call(
        kernel, "image",
        [(ext, rows, cols), (mid, rows, cols), (mid, rows, cols)], 3,
        [(2, ext, rows, cols)], 400_000_000,
    )


def build_force(depth, rows, cols, groups):
    ext, mid = depth + 2 * EDGE, depth + 2 * SMOOTH

    def kernel(warped, image, mean, variance, force, boxes, slope):
        box = band(cols, WIN)
        first = jnp.concatenate([box, column_difference(cols)], axis=1).astype(bf16)
        box = box.astype(bf16)
        twice = jnp.concatenate([box, box], axis=0)

        def columns(i, carry):
            at = pl.ds(i * CHUNK, CHUNK)
            one, two = flat(warped[at]), flat(image[at])
            both = jnp.dot(one.astype(bf16), first, preferred_element_type=f32)
            results = [both[:, :cols], square_columns(one * one, twice), square_columns(one * two, twice)]
            for field, result in enumerate(results):
                boxes[field, at] = result.reshape(CHUNK, rows, cols)
            slope[at] = both[:, cols:].reshape(CHUNK, rows, cols)
            return carry

        lax.fori_loop(0, ext // CHUNK, columns, 0)
        row = lax.broadcasted_iota(jnp.int32, (rows, cols), 0)

        def local(i, carry):
            start = i * STEP
            means = [
                [row_window(v, row) * SCALE for v in z_windows(lambda k: boxes[f, start + k], STEP)]
                for f in range(3)
            ]
            for k in range(STEP):
                mi, mii, mij = [field[k] for field in means]
                mj, var_j = mean[start + k], variance[start + k]
                at = start + k + WIN
                centre = warped[at]
                var_i = mii - mi * mi
                cov = mij - mi * mj
                factor = (image[at] - mj - cov / (var_i + epsilon) * (centre - mi)) / jnp.sqrt(
                    var_i * var_j + epsilon
                )
                grad_z = 0.5 * (warped[at + 1] - warped[at - 1])
                below = jnp.where(row < rows - 1, pltpu.roll(centre, rows - 1, 0), 0.0)
                above = jnp.where(row > 0, pltpu.roll(centre, 1, 0), 0.0)
                force[0, start + k] = factor * grad_z
                force[1, start + k] = factor * (0.5 * (below - above))
                force[2, start + k] = factor * slope[at]
            return carry

        lax.fori_loop(0, mid // STEP, local, 0)

        @pl.when(lax.axis_index("gz") == 0)
        def _():
            force[:, 0:SMOOTH] = jnp.zeros((3, SMOOTH, rows, cols), f32)

        @pl.when(lax.axis_index("gz") == groups - 1)
        def _():
            force[:, mid - SMOOTH : mid] = jnp.zeros((3, SMOOTH, rows, cols), f32)

    return local_call(
        kernel, "force", [(3, mid, rows, cols)], 4,
        [(3, ext, rows, cols), (ext, rows, cols)], 1_000_000_000,
    )


def build_smooth(depth, rows, cols):
    def kernel(force, velocity, padded):
        g_high, g_low = split(gauss_columns(cols))
        g_all = jnp.concatenate(
            [
                jnp.concatenate([g_high, g_low], axis=1),
                jnp.concatenate([g_high, jnp.zeros_like(g_low)], axis=1),
            ],
            axis=0,
        )
        padded[...] = jnp.zeros(padded.shape, f32)

        def finish(i, carry):
            start = i * STEP
            for axis in range(3):
                x = [force[axis, start + k] for k in range(STEP + 2 * SMOOTH)]
                for k in range(STEP):
                    value = GAUSS[0] * x[k + SMOOTH]
                    for d in range(1, SMOOTH + 1):
                        value = value + GAUSS[d] * (x[k + SMOOTH - d] + x[k + SMOOTH + d])
                    padded[axis, k, SMOOTH : SMOOTH + rows] = value
                mixed = GAUSS[0] * padded[axis, :, SMOOTH : SMOOTH + rows]
                for d in range(1, SMOOTH + 1):
                    mixed = mixed + GAUSS[d] * (
                        padded[axis, :, SMOOTH - d : SMOOTH - d + rows]
                        + padded[axis, :, SMOOTH + d : SMOOTH + d + rows]
                    )
                pair = jnp.concatenate(split(flat(mixed)), axis=1)
                done = jnp.dot(pair, g_all, preferred_element_type=f32)
                velocity[axis, pl.ds(start, STEP)] = (done[:, :cols] + done[:, cols:]).reshape(
                    STEP, rows, cols
                )
            return carry

        lax.fori_loop(0, depth // STEP, finish, 0)

    return local_call(
        kernel, "smooth", [(3, depth, rows, cols)], 1,
        [(3, STEP, rows + 2 * SMOOTH, cols)], 600_000_000,
    )


def per_device(template, subjects, shifts, fractions):
    groups = lax.axis_size("gz")
    members = lax.axis_size("subj")
    subject_count, depth, rows, cols = subjects.shape
    share = depth // members
    reach = -(-HALO // share)
    me = lax.axis_index("subj")
    bits = bits_of(members)[2:]
    subject, shift, fraction = subjects[0], shifts[0], fractions[0]

    arrived = swap(template, "subj", bits[-1])
    to_near, to_far, mine = build_pack(depth, rows, cols, share)(
        template, shift, fraction, subject
    )
    pieces = jnp.concatenate([mine, arrived], axis=0)
    pieces, to_near, to_far = lax.optimization_barrier((pieces, to_near, to_far))
    near_m, far_m = swap_near(to_near, "gz"), swap_far(to_far, "gz")
    for bit in bits[-2::-1]:
        pieces = jnp.concatenate([pieces, swap(pieces, "subj", bit)], axis=0)
    pieces = jnp.concatenate(
        [pieces] + [swap(pieces, "subj", k) for k in range(1, PEERS)], axis=0
    )

    def shares(numbers):
        starts = [place_of_shard(me, number, members) * share for number in numbers]
        return jnp.concatenate(
            [lax.dynamic_slice_in_dim(pieces, start, share, 0) for start in starts], axis=0
        )

    low_t = shares(range(reach))[:HALO]
    high_t = shares(range(members - reach, members))[-HALO:]
    to_near, to_far = at_ends("gz", low_t, high_t)
    near_t, far_t = swap_near(to_near, "gz"), swap_far(to_far, "gz")

    (inner,) = build_inner_warp(depth, rows, cols, members)(pieces, shift, fraction)
    warped, keep, *sends = build_outer_warp(depth, rows, cols, members, groups)(
        low_t, high_t, near_t, far_t, near_m, far_m, shift, fraction, subject, inner
    )

    parts = [swap(send, "subj", k) for k, send in zip(range(1, PEERS), sends)]
    near_m, far_m, subject, warped = lax.optimization_barrier((near_m, far_m, subject, warped))
    image, mean, variance = build_image(depth, rows, cols, groups)(near_m, far_m, subject)
    (force,) = build_force(depth, rows, cols, groups)(warped, image, mean, variance)
    *parts, force = lax.optimization_barrier((*parts, force))
    keep = keep + parts[0] + parts[1] + parts[2]
    for bit in bits:
        pairs = keep.reshape((-1, 2, share) + keep.shape[1:])
        keep, send = [pairs[:, part].reshape((-1,) + keep.shape[1:]) for part in (0, 1)]
        keep = keep + swap(send, "subj", bit)
    (velocity,) = build_smooth(depth, rows, cols)(force)
    template_force = keep * (1.0 / math.sqrt(subject_count * members))
    return (velocity[None], template_force)


def solution(mesh):
    placed = (
        P(("gz", "subj"), None, None),
        P("subj", "gz", None, None),
        P("subj", None, "gz", None, None),
        P("subj", None, "gz", None, None),
    )
    return jax.shard_map(
        per_device,
        mesh=mesh,
        in_specs=placed,
        out_specs=(P("subj", None, "gz", None, None), P(("gz", "subj"), None, None)),
        check_vma=False,
    )
```

```python
import math

import jax
import jax.numpy as jnp
from jax import lax
from jax.experimental import pallas as pl
from jax.experimental.pallas import tpu as pltpu
from jax.sharding import PartitionSpec as P

SHIFT = 2
WIN = 4
SMOOTH = 4
EDGE = WIN + SMOOTH
HALO = EDGE + SHIFT + 1
TAPS = 2 * SHIFT + 2
sigma = 1.5
epsilon = 1e-05
f32 = jnp.float32
bf16 = jnp.bfloat16
PEERS = 4
ORDER = (0, 1, 3, 2)
VMEM_LIMIT = 48 * 1024 * 1024

raw = [math.exp(-k * k / (2 * sigma * sigma)) for k in range(SMOOTH + 1)]
norm = raw[0] + 2 * sum(raw[1:])
GAUSS = [value / norm for value in raw]


def swap(block, axis, bit):
    count = lax.axis_size(axis)
    return lax.ppermute(block, axis, [(i, i ^ bit) for i in range(count)])


def swap_near(block, axis):
    count = lax.axis_size(axis)
    pairs = [(i, i ^ 1) for i in range(count) if (i ^ 1) < count]
    return lax.ppermute(block, axis, pairs)


def swap_far(block, axis):
    count = lax.axis_size(axis)
    assert count % 2 == 0
    return lax.ppermute(
        block, axis, [(i, (i + 1 if i % 2 else i - 1) % count) for i in range(count)]
    )


def has_far(group, groups):
    return (group != 0) & (group != groups - 1)


def bits_of(count):
    return [1 << place for place in range(count.bit_length() - 1)]


def mirrored(number, count):
    places = count.bit_length() - 1
    return sum(((number >> place) & 1) << (places - 1 - place) for place in range(places))


def at_ends(axis, low, high):
    odd = lax.axis_index(axis) % 2 == 1
    return jnp.where(odd, low, high), jnp.where(odd, high, low)


def shift_matrix(offsets, cols):
    source = lax.broadcasted_iota(jnp.int32, (cols, cols), 0)
    target = lax.broadcasted_iota(jnp.int32, (cols, cols), 1)
    return jnp.concatenate(
        [(source == target + offset).astype(f32) for offset in offsets], axis=1
    ).astype(bf16)


def rows_at(value, index):
    return jnp.take_along_axis(value, index, axis=0, mode="promise_in_bounds")


def even_odd(base, frac):
    even = (base & 1) == 0
    rest = 1.0 - frac
    return jnp.where(even, rest, frac), jnp.where(even, frac, rest)


def warp_slice(shifted, plane, sz, sr, sc, fz, fr, fc):
    rows = sz.shape[0]
    row = lax.broadcasted_iota(jnp.int32, sz.shape, 0) + sr
    after = row + 1
    index0, index1 = row & (rows - 1), after & (rows - 1)
    weight0 = jnp.where(index0 == row, 1.0 - fr, 0.0)
    weight1 = jnp.where(index1 == after, fr, 0.0)
    col_e, col_o = even_odd(sc, fc)
    dep_e, dep_o = even_odd(sz, fz)
    picks = {k: (sc >= k - 3, sz >= k - 3) for k in range(2, TAPS)}
    planes = [None, None]
    for kz in range(TAPS):
        corner = [[None, None], [None, None]]
        for kc in range(TAPS):
            value = shifted[kc, plane + kz]
            for b, index in ((0, index0), (1, index1)):
                taken = rows_at(value, index)
                if kc < 2:
                    corner[b][kc] = taken
                else:
                    corner[b][kc % 2] = jnp.where(picks[kc][0], taken, corner[b][kc % 2])
        flat = corner[0] + corner[1]
        if kz < 2:
            planes[kz] = flat
        else:
            mask = picks[kz][1]
            planes[kz % 2] = [jnp.where(mask, new, old) for new, old in zip(flat, planes[kz % 2])]
    parts = []
    for e0, o0, e1, o1 in planes:
        parts.append(
            weight0 * (col_e * e0 + col_o * o0) + weight1 * (col_e * e1 + col_o * o1)
        )
    summed = dep_e * parts[0] + dep_o * parts[1]
    return summed.astype(bf16).astype(f32)


def move_columns(slab, shifted, start, step):
    rows, cols = slab.shape[1:]
    offsets = [k - SHIFT for k in range(TAPS) if k != SHIFT]
    matrix = shift_matrix(offsets, cols)
    block = slab[start : start + step]
    shifted[SHIFT, start : start + step] = block
    moved = jnp.dot(
        block.reshape(step * rows, cols).astype(bf16), matrix, preferred_element_type=f32
    )
    for number, offset in enumerate(offsets):
        shifted[offset + SHIFT, start : start + step] = moved[
            :, number * cols : (number + 1) * cols
        ].reshape(step, rows, cols)


def vmem_specs(count):
    return [pl.BlockSpec(memory_space=pltpu.VMEM)] * count


def local_call(kernel, name, outs, inputs, scratch, flops):
    return pl.pallas_call(
        kernel,
        out_shape=[jax.ShapeDtypeStruct(shape, f32) for shape in outs],
        in_specs=vmem_specs(inputs),
        out_specs=vmem_specs(len(outs)),
        scratch_shapes=[pltpu.VMEM(shape, f32) for shape in scratch],
        compiler_params=pltpu.CompilerParams(vmem_limit_bytes=VMEM_LIMIT),
        cost_estimate=pl.CostEstimate(flops=flops, bytes_accessed=8_000_000, transcendentals=0),
        name=name,
    )


def slice_fields(shifts, fractions, z):
    return [shifts[axis, z] for axis in range(3)] + [
        fractions[axis, z].astype(f32) for axis in range(3)
    ]


def place_of_shard(me, shard, members):
    apart = me ^ shard
    quarter = members // PEERS
    peer = apart & (PEERS - 1)
    block = sum(jnp.where(peer == k, c, 0) for c, k in enumerate(ORDER))
    return block * quarter + mirrored(apart // PEERS, quarter)


def build_pack(depth, rows, cols, share):
    def kernel(template, shifts, fractions, subjects, near, far, mine, whole, parts, done):
        odd = lax.axis_index("gz") % 2 == 1
        starts = (0, depth - EDGE)
        copies = [pltpu.make_async_copy(template, mine, done.at[6])]
        for end, start in enumerate(starts):
            at = pl.ds(start, EDGE)
            copies.append(pltpu.make_async_copy(shifts.at[:, at], whole.at[end], done.at[3 * end]))
            copies.append(
                pltpu.make_async_copy(fractions.at[:, at], parts.at[end, 0:3], done.at[3 * end + 1])
            )
            copies.append(
                pltpu.make_async_copy(subjects.at[at], parts.at[end, 3], done.at[3 * end + 2])
            )
        for copy in copies:
            copy.start()
        for copy in copies:
            copy.wait()
        for axis in range(7):
            if axis < 3:
                low, high = whole[0, axis].astype(f32), whole[1, axis].astype(f32)
            else:
                low, high = parts[0, axis - 3].astype(f32), parts[1, axis - 3].astype(f32)
            near[axis] = jnp.where(odd, low, high).astype(bf16)
            far[axis] = jnp.where(odd, high, low).astype(bf16)

    any_spec = pl.BlockSpec(memory_space=pl.ANY)
    message = jax.ShapeDtypeStruct((7, EDGE, rows, cols), bf16)
    return pl.pallas_call(
        kernel,
        out_shape=[message, message, jax.ShapeDtypeStruct((share, rows, cols), bf16)],
        in_specs=[any_spec] * 4,
        out_specs=vmem_specs(3),
        scratch_shapes=[
            pltpu.VMEM((2, 3, EDGE, rows, cols), jnp.int32),
            pltpu.VMEM((2, 4, EDGE, rows, cols), bf16),
            pltpu.SemaphoreType.DMA((7,)),
        ],
        compiler_params=pltpu.CompilerParams(vmem_limit_bytes=VMEM_LIMIT),
        cost_estimate=pl.CostEstimate(flops=1_000_000, bytes_accessed=2_000_000, transcendentals=0),
        name="pack",
    )


def peer_shard(i, me, share, members, first):
    quarter = members // PEERS
    block = i // share
    return (me ^ (first + block // quarter + PEERS * (block % quarter))) * share + i % share


def end_slices(depth):
    return [*range(SHIFT), *range(depth - SHIFT - 1, depth)]


def build_inner_warp(depth, rows, cols, members):
    share = depth // members
    away = depth - depth // PEERS
    front, count = SHIFT, depth + 2 * SHIFT + 2

    def kernel(pieces, shifts, fractions, subjects, sent, send, shifted, slab):
        me = lax.axis_index("subj")
        quarter = members // PEERS
        slab[0:front] = jnp.zeros((front, rows, cols), f32)
        slab[front + depth : count] = jnp.zeros((count - front - depth, rows, cols), f32)
        for k in range(members):
            shard = me ^ (ORDER[k // quarter] + PEERS * mirrored(k % quarter, quarter))
            slab[pl.ds(front + shard * share, share)] = pieces[k * share : (k + 1) * share].astype(f32)
        for start in range(0, count, count // 2):
            move_columns(slab, shifted, start, count // 2)

        def body(i, carry):
            z = peer_shard(i, me, share, members, 1)
            out = warp_slice(shifted, front + z - SHIFT, *slice_fields(shifts, fractions, z))
            sent[i] = out
            send[i] = subjects[z].astype(f32) - out
            return carry

        lax.fori_loop(0, away, body, 0, unroll=6)

    part = (away, rows, cols)
    return local_call(
        kernel, "inner_warp", [part, part, (TAPS, count, rows, cols)], 4,
        [(count, rows, cols)], 1_000_000_000,
    )


def build_end_warp(depth, rows, cols, members, groups):
    share = depth // members
    quarter, kept = members // PEERS, depth // PEERS
    away = depth - kept
    inner = SHIFT + EDGE
    planes = HALO + inner

    def kernel(
        low_t, high_t, near_t, far_t, shifts, fractions, subjects, send_in, *outs_and_scratch
    ):
        *sends, ends, shifted, slab = outs_and_scratch
        odd = lax.axis_index("gz") % 2 == 1
        me = lax.axis_index("subj")
        inside = has_far(lax.axis_index("gz"), groups)
        near, far = near_t[...].astype(f32), jnp.where(inside, far_t[...].astype(f32), 0.0)
        slab[0:HALO] = jnp.where(odd, near, far)
        slab[HALO:planes] = low_t[0:inner].astype(f32)
        slab[planes : planes + inner] = high_t[HALO - inner : HALO].astype(f32)
        slab[planes + inner : 2 * planes] = jnp.where(odd, far, near)
        move_columns(slab, shifted, 0, 2 * planes)
        for number, send in enumerate(sends):
            send[...] = send_in[number * kept : (number + 1) * kept]
        for number, z in enumerate(end_slices(depth)):
            plane = HALO + z if z < SHIFT else 2 * planes - HALO - depth + z
            out = warp_slice(shifted, plane - SHIFT, *slice_fields(shifts, fractions, z))
            ends[number] = out
            residual = subjects[z].astype(f32) - out
            apart = me ^ (z // share)
            index = (apart // PEERS) * share + z % share
            for k, send in enumerate(sends, 1):

                @pl.when(apart % PEERS == k)
                def _():
                    send[index] = residual

    part = (kept, rows, cols)
    count = len(end_slices(depth))
    return local_call(
        kernel, "end_warp",
        [part] * (PEERS - 1) + [(count, rows, cols), (TAPS, 2 * planes, rows, cols)], 8,
        [(2 * planes, rows, cols)], 300_000_000,
    )


def build_rest_warp(depth, rows, cols, members, groups):
    share = depth // members
    kept = depth // PEERS
    planes = HALO + SHIFT + EDGE

    def kernel(
        moved, moved_ends, sent, ends, near_m, far_m, shifts, fractions, subjects, warped, keep
    ):
        me = lax.axis_index("subj")
        odd = lax.axis_index("gz") % 2 == 1
        inside = has_far(lax.axis_index("gz"), groups)

        def body(i, carry):
            z = peer_shard(i, me, share, members, 0)
            out = warp_slice(moved, z, *slice_fields(shifts, fractions, z))
            warped[EDGE + z] = out
            keep[i] = subjects[z].astype(f32) - out
            for part in range(PEERS - 1):
                number = part * kept + i
                warped[EDGE + peer_shard(number, me, share, members, 1)] = sent[number]
            return carry

        lax.fori_loop(0, kept, body, 0, unroll=4)
        for number, z in enumerate(end_slices(depth)):
            out = ends[number]
            warped[EDGE + z] = out
            apart = me ^ (z // share)

            @pl.when(apart % PEERS == 0)
            def _():
                keep[(apart // PEERS) * share + z % share] = subjects[z].astype(f32) - out

        def outside(z, carry):
            for low in (True, False):
                fields = []
                for axis in range(6):
                    one = near_m[axis, z].astype(f32)
                    two = jnp.where(inside, far_m[axis, z].astype(f32), 0.0)
                    field = jnp.where(odd, one, two) if low else jnp.where(odd, two, one)
                    fields.append(field.astype(jnp.int32) if axis < 3 else field)
                plane = HALO - EDGE + z if low else 2 * planes - HALO + z
                warped[z if low else depth + EDGE + z] = warp_slice(
                    moved_ends, plane - SHIFT, *fields
                )
            return carry

        lax.fori_loop(0, EDGE, outside, 0, unroll=2)

    return local_call(
        kernel, "rest_warp", [(depth + 2 * EDGE, rows, cols), (kept, rows, cols)], 9, [],
        600_000_000,
    )


def band(cols, radius):
    apart = jnp.abs(
        lax.broadcasted_iota(jnp.int32, (cols, cols), 0)
        - lax.broadcasted_iota(jnp.int32, (cols, cols), 1)
    )
    return (apart <= radius).astype(f32)


def column_difference(cols):
    apart = lax.broadcasted_iota(jnp.int32, (cols, cols), 0) - lax.broadcasted_iota(
        jnp.int32, (cols, cols), 1
    )
    return jnp.where(apart == 1, 0.5, jnp.where(apart == -1, -0.5, 0.0)).astype(f32)


def gauss_columns(cols):
    apart = jnp.abs(
        lax.broadcasted_iota(jnp.int32, (cols, cols), 0)
        - lax.broadcasted_iota(jnp.int32, (cols, cols), 1)
    )
    result = jnp.zeros((cols, cols), f32)
    for k, tap in enumerate(GAUSS):
        result = jnp.where(apart == k, f32(tap), result)
    return result


def split(value):
    high = value.astype(bf16)
    return high, (value - high.astype(f32)).astype(bf16)


def take_rows(value, index):
    return jnp.take_along_axis(value, index, axis=0, mode="promise_in_bounds")


def row_window(value, row):
    first = row < WIN
    half = value + take_rows(value, row ^ 1)
    half = half + take_rows(half, row ^ 2)
    outer = jnp.clip(jnp.where(first, row - 1, row + 1), 0, 2 * WIN - 1)
    outer_two = jnp.clip(jnp.where(first, row - 2, row + 2), 0, 2 * WIN - 1)
    reach = jnp.where(first, row, 2 * WIN - 1 - row)
    across = take_rows(value, row ^ WIN) + jnp.where(
        reach >= 1, take_rows(value, outer ^ WIN), 0.0
    )
    return half + across + jnp.where(reach >= 2, take_rows(across, outer_two), 0.0)


def z_windows(load, count):
    x = [load(k) for k in range(count + 2 * WIN)]
    two = [x[k] + x[k + 1] for k in range(count + 2 * WIN - 1)]
    four = [two[k] + two[k + 2] for k in range(count + 2 * WIN - 3)]
    return [four[k] + four[k + 4] + x[k + 8] for k in range(count)]


STEP = 8
CHUNK = 16
PART = 32
SCALE = 1.0 / float((2 * WIN + 1) ** 3)


def flat(value):
    return value.reshape(-1, value.shape[-1])


def square_columns(product, twice):
    pair = jnp.concatenate(split(product), axis=1)
    return jnp.dot(pair, twice, preferred_element_type=f32)


def build_image(depth, rows, cols, groups):
    ext, mid = depth + 2 * EDGE, depth + 2 * SMOOTH

    def kernel(near_m, far_m, subjects, image, mean, variance, boxes):
        odd = lax.axis_index("gz") % 2 == 1
        near = near_m[6].astype(f32)
        far = jnp.where(has_far(lax.axis_index("gz"), groups), far_m[6].astype(f32), 0.0)
        image[0:EDGE] = jnp.where(odd, near, far)
        image[EDGE : EDGE + depth] = subjects[...].astype(f32)
        image[EDGE + depth : ext] = jnp.where(odd, far, near)
        box = band(cols, WIN).astype(bf16)
        twice = jnp.concatenate([box, box], axis=0)

        def columns(i, carry):
            at = pl.ds(i * CHUNK, CHUNK)
            two = flat(image[at])
            results = [
                jnp.dot(two.astype(bf16), box, preferred_element_type=f32),
                square_columns(two * two, twice),
            ]
            for field, result in enumerate(results):
                boxes[field, at] = result.reshape(CHUNK, rows, cols)
            return carry

        lax.fori_loop(0, ext // CHUNK, columns, 0, unroll=True)
        row = lax.broadcasted_iota(jnp.int32, (rows, cols), 0)

        def local(i, carry):
            start = i * STEP
            one, two = [
                [row_window(v, row) * SCALE for v in z_windows(lambda k: boxes[f, start + k], STEP)]
                for f in range(2)
            ]
            for k in range(STEP):
                mean[start + k] = one[k]
                variance[start + k] = two[k] - one[k] * one[k]
            return carry

        lax.fori_loop(0, mid // STEP, local, 0, unroll=True)

    return local_call(
        kernel, "image",
        [(ext, rows, cols), (mid, rows, cols), (mid, rows, cols)], 3,
        [(2, ext, rows, cols)], 400_000_000,
    )


def build_force(depth, rows, cols, groups):
    ext, mid = depth + 2 * EDGE, depth + 2 * SMOOTH

    def kernel(warped, image, mean, variance, force, boxes, slope):
        box = band(cols, WIN)
        first = jnp.concatenate([box, column_difference(cols)], axis=1).astype(bf16)
        box = box.astype(bf16)
        twice = jnp.concatenate([box, box], axis=0)

        def columns(i, carry):
            at = pl.ds(i * CHUNK, CHUNK)
            one, two = flat(warped[at]), flat(image[at])
            both = jnp.dot(one.astype(bf16), first, preferred_element_type=f32)
            results = [both[:, :cols], square_columns(one * one, twice), square_columns(one * two, twice)]
            for field, result in enumerate(results):
                boxes[field, at] = result.reshape(CHUNK, rows, cols)
            slope[at] = both[:, cols:].reshape(CHUNK, rows, cols)
            return carry

        lax.fori_loop(0, ext // CHUNK, columns, 0, unroll=True)
        row = lax.broadcasted_iota(jnp.int32, (rows, cols), 0)

        def local(i, carry):
            start = i * STEP
            means = [
                [row_window(v, row) * SCALE for v in z_windows(lambda k: boxes[f, start + k], STEP)]
                for f in range(3)
            ]
            for k in range(STEP):
                mi, mii, mij = [field[k] for field in means]
                mj, var_j = mean[start + k], variance[start + k]
                at = start + k + WIN
                centre = warped[at]
                var_i = mii - mi * mi
                cov = mij - mi * mj
                factor = (image[at] - mj - cov / (var_i + epsilon) * (centre - mi)) / jnp.sqrt(
                    var_i * var_j + epsilon
                )
                grad_z = 0.5 * (warped[at + 1] - warped[at - 1])
                below = jnp.where(row < rows - 1, pltpu.roll(centre, rows - 1, 0), 0.0)
                above = jnp.where(row > 0, pltpu.roll(centre, 1, 0), 0.0)
                force[0, start + k] = factor * grad_z
                force[1, start + k] = factor * (0.5 * (below - above))
                force[2, start + k] = factor * slope[at]
            return carry

        lax.fori_loop(0, mid // STEP, local, 0, unroll=True)

        @pl.when(lax.axis_index("gz") == 0)
        def _():
            force[:, 0:SMOOTH] = jnp.zeros((3, SMOOTH, rows, cols), f32)

        @pl.when(lax.axis_index("gz") == groups - 1)
        def _():
            force[:, mid - SMOOTH : mid] = jnp.zeros((3, SMOOTH, rows, cols), f32)

    return local_call(
        kernel, "force", [(3, mid, rows, cols)], 4,
        [(3, ext, rows, cols), (ext, rows, cols)], 1_000_000_000,
    )


def build_smooth(depth, rows, cols):
    chunks = depth // PART

    def kernel(force, velocity, padded, result, done):
        g_high, g_low = split(gauss_columns(cols))
        g_all = jnp.concatenate(
            [
                jnp.concatenate([g_high, g_low], axis=1),
                jnp.concatenate([g_high, jnp.zeros_like(g_low)], axis=1),
            ],
            axis=0,
        )
        padded[...] = jnp.zeros(padded.shape, f32)

        def sent(i):
            at = pl.ds(i * PART, PART)
            return pltpu.make_async_copy(result.at[:, at], velocity.at[:, at], done.at[i])

        def finish(i, carry):
            start = i * PART
            for axis in range(3):
                x = [force[axis, start + k] for k in range(PART + 2 * SMOOTH)]
                for k in range(PART):
                    value = GAUSS[0] * x[k + SMOOTH]
                    for d in range(1, SMOOTH + 1):
                        value = value + GAUSS[d] * (x[k + SMOOTH - d] + x[k + SMOOTH + d])
                    padded[axis, k, SMOOTH : SMOOTH + rows] = value
                highs, lows = [], []
                for k in range(0, PART, 2):
                    both = []
                    for n in (k, k + 1):
                        value = GAUSS[0] * padded[axis, n, SMOOTH : SMOOTH + rows]
                        for d in range(1, SMOOTH + 1):
                            value = value + GAUSS[d] * (
                                padded[axis, n, SMOOTH - d : SMOOTH - d + rows]
                                + padded[axis, n, SMOOTH + d : SMOOTH + d + rows]
                            )
                        both.append(value)
                    high, low = split(jnp.concatenate(both, axis=0))
                    highs.append(high)
                    lows.append(low)
                pair = jnp.concatenate(
                    [jnp.concatenate(highs, axis=0), jnp.concatenate(lows, axis=0)], axis=1
                )
                mixed = jnp.dot(pair, g_all, preferred_element_type=f32)
                result[axis, pl.ds(start, PART)] = (mixed[:, :cols] + mixed[:, cols:]).reshape(
                    PART, rows, cols
                )
            sent(i).start()
            return carry

        lax.fori_loop(0, chunks, finish, 0, unroll=True)
        for i in range(chunks):
            sent(i).wait()

    return pl.pallas_call(
        kernel,
        out_shape=[jax.ShapeDtypeStruct((3, depth, rows, cols), f32)],
        in_specs=vmem_specs(1),
        out_specs=[pl.BlockSpec(memory_space=pl.ANY)],
        scratch_shapes=[
            pltpu.VMEM((3, PART, rows + 2 * SMOOTH, cols), f32),
            pltpu.VMEM((3, depth, rows, cols), f32),
            pltpu.SemaphoreType.DMA((chunks,)),
        ],
        compiler_params=pltpu.CompilerParams(vmem_limit_bytes=VMEM_LIMIT),
        cost_estimate=pl.CostEstimate(flops=600_000_000, bytes_accessed=8_000_000, transcendentals=0),
        name="smooth",
    )


def per_device(template, subjects, shifts, fractions):
    groups = lax.axis_size("gz")
    members = lax.axis_size("subj")
    subject_count, depth, rows, cols = subjects.shape
    share = depth // members
    reach = -(-HALO // share)
    me = lax.axis_index("subj")
    bits = bits_of(members)[2:]
    subject, shift, fraction = subjects[0], shifts[0], fractions[0]

    arrived = swap(template, "subj", bits[-1])
    to_near, to_far, mine = build_pack(depth, rows, cols, share)(
        template, shift, fraction, subject
    )
    pieces = jnp.concatenate([mine, arrived], axis=0)
    pieces, to_near, to_far = lax.optimization_barrier((pieces, to_near, to_far))
    near_m, far_m = swap_near(to_near, "gz"), swap_far(to_far, "gz")
    for bit in bits[-2::-1]:
        pieces = jnp.concatenate([pieces, swap(pieces, "subj", bit)], axis=0)
    pieces = jnp.concatenate(
        [pieces] + [swap(pieces, "subj", k) for k in ORDER[1:]], axis=0
    )

    def shares(numbers):
        starts = [place_of_shard(me, number, members) * share for number in numbers]
        return jnp.concatenate(
            [lax.dynamic_slice_in_dim(pieces, start, share, 0) for start in starts], axis=0
        )

    low_t = shares(range(reach))[:HALO]
    high_t = shares(range(members - reach, members))[-HALO:]
    to_near, to_far = at_ends("gz", low_t, high_t)
    near_t, far_t = swap_near(to_near, "gz"), swap_far(to_far, "gz")

    sent, send, moved = build_inner_warp(depth, rows, cols, members)(pieces, shift, fraction, subject)
    *sends, ends, moved_ends = build_end_warp(depth, rows, cols, members, groups)(
        low_t, high_t, near_t, far_t, shift, fraction, subject, send
    )

    parts = [swap(sends[k - 1], "subj", k) for k in (3, 1, 2)]
    warped, keep = build_rest_warp(depth, rows, cols, members, groups)(
        moved, moved_ends, sent, ends, near_m, far_m, shift, fraction, subject
    )
    near_m, far_m, subject, warped = lax.optimization_barrier((near_m, far_m, subject, warped))
    image, mean, variance = build_image(depth, rows, cols, groups)(near_m, far_m, subject)
    (force,) = build_force(depth, rows, cols, groups)(warped, image, mean, variance)
    *parts, force = lax.optimization_barrier((*parts, force))
    keep = keep + parts[0] + parts[1] + parts[2]
    for bit in bits:
        pairs = keep.reshape((-1, 2, share) + keep.shape[1:])
        keep, send = [pairs[:, part].reshape((-1,) + keep.shape[1:]) for part in (0, 1)]
        keep = keep + swap(send, "subj", bit)
    (velocity,) = build_smooth(depth, rows, cols)(force)
    template_force = keep * (1.0 / math.sqrt(subject_count * members))
    return (velocity[None], template_force)


def solution(mesh):
    placed = (
        P(("gz", "subj"), None, None),
        P("subj", "gz", None, None),
        P("subj", None, "gz", None, None),
        P("subj", None, "gz", None, None),
    )
    return jax.shard_map(
        per_device,
        mesh=mesh,
        in_specs=placed,
        out_specs=(P("subj", None, "gz", None, None), P(("gz", "subj"), None, None)),
        check_vma=False,
    )
```

```python
import math

import jax
import jax.numpy as jnp
from jax import lax
from jax.experimental import pallas as pl
from jax.experimental.pallas import tpu as pltpu
from jax.sharding import PartitionSpec as P

SHIFT = 2
WIN = 4
SMOOTH = 4
EDGE = WIN + SMOOTH
HALO = EDGE + SHIFT + 1
TAPS = 2 * SHIFT + 2
sigma = 1.5
epsilon = 1e-05
f32 = jnp.float32
bf16 = jnp.bfloat16
PEERS = 4
ORDER = (0, 1, 3, 2)
VMEM_LIMIT = 48 * 1024 * 1024

raw = [math.exp(-k * k / (2 * sigma * sigma)) for k in range(SMOOTH + 1)]
norm = raw[0] + 2 * sum(raw[1:])
GAUSS = [value / norm for value in raw]


def swap(block, axis, bit):
    count = lax.axis_size(axis)
    return lax.ppermute(block, axis, [(i, i ^ bit) for i in range(count)])


def swap_near(block, axis):
    count = lax.axis_size(axis)
    pairs = [(i, i ^ 1) for i in range(count) if (i ^ 1) < count]
    return lax.ppermute(block, axis, pairs)


def swap_far(block, axis):
    count = lax.axis_size(axis)
    assert count % 2 == 0
    return lax.ppermute(
        block, axis, [(i, (i + 1 if i % 2 else i - 1) % count) for i in range(count)]
    )


def has_far(group, groups):
    return (group != 0) & (group != groups - 1)


def bits_of(count):
    return [1 << place for place in range(count.bit_length() - 1)]


def mirrored(number, count):
    places = count.bit_length() - 1
    return sum(((number >> place) & 1) << (places - 1 - place) for place in range(places))


def at_ends(axis, low, high):
    odd = lax.axis_index(axis) % 2 == 1
    return jnp.where(odd, low, high), jnp.where(odd, high, low)


def shift_matrix(offsets, cols):
    source = lax.broadcasted_iota(jnp.int32, (cols, cols), 0)
    target = lax.broadcasted_iota(jnp.int32, (cols, cols), 1)
    return jnp.concatenate(
        [(source == target + offset).astype(f32) for offset in offsets], axis=1
    ).astype(bf16)


def rows_at(value, index):
    return jnp.take_along_axis(value, index, axis=0, mode="promise_in_bounds")


def even_odd(base, frac):
    even = (base & 1) == 0
    rest = 1.0 - frac
    return jnp.where(even, rest, frac), jnp.where(even, frac, rest)


def warp_slice(shifted, plane, sz, sr, sc, fz, fr, fc):
    rows = sz.shape[0]
    row = lax.broadcasted_iota(jnp.int32, sz.shape, 0) + sr
    after = row + 1
    index0, index1 = row & (rows - 1), after & (rows - 1)
    weight0 = jnp.where(index0 == row, 1.0 - fr, 0.0)
    weight1 = jnp.where(index1 == after, fr, 0.0)
    col_e, col_o = even_odd(sc, fc)
    dep_e, dep_o = even_odd(sz, fz)
    picks = {k: (sc >= k - 3, sz >= k - 3) for k in range(2, TAPS)}
    planes = [None, None]
    for kz in range(TAPS):
        corner = [[None, None], [None, None]]
        for kc in range(TAPS):
            value = shifted[kc, plane + kz]
            for b, index in ((0, index0), (1, index1)):
                taken = rows_at(value, index)
                if kc < 2:
                    corner[b][kc] = taken
                else:
                    corner[b][kc % 2] = jnp.where(picks[kc][0], taken, corner[b][kc % 2])
        flat = corner[0] + corner[1]
        if kz < 2:
            planes[kz] = flat
        else:
            mask = picks[kz][1]
            planes[kz % 2] = [jnp.where(mask, new, old) for new, old in zip(flat, planes[kz % 2])]
    parts = []
    for e0, o0, e1, o1 in planes:
        parts.append(
            weight0 * (col_e * e0 + col_o * o0) + weight1 * (col_e * e1 + col_o * o1)
        )
    summed = dep_e * parts[0] + dep_o * parts[1]
    return summed.astype(bf16).astype(f32)


def move_columns(slab, shifted, start, step):
    rows, cols = slab.shape[1:]
    offsets = [k - SHIFT for k in range(TAPS) if k != SHIFT]
    matrix = shift_matrix(offsets, cols)
    block = slab[start : start + step]
    shifted[SHIFT, start : start + step] = block
    moved = jnp.dot(
        block.reshape(step * rows, cols).astype(bf16), matrix, preferred_element_type=f32
    )
    for number, offset in enumerate(offsets):
        shifted[offset + SHIFT, start : start + step] = moved[
            :, number * cols : (number + 1) * cols
        ].reshape(step, rows, cols)


def vmem_specs(count):
    return [pl.BlockSpec(memory_space=pltpu.VMEM)] * count


def local_call(kernel, name, outs, inputs, scratch, flops):
    return pl.pallas_call(
        kernel,
        out_shape=[jax.ShapeDtypeStruct(shape, f32) for shape in outs],
        in_specs=vmem_specs(inputs),
        out_specs=vmem_specs(len(outs)),
        scratch_shapes=[pltpu.VMEM(shape, f32) for shape in scratch],
        compiler_params=pltpu.CompilerParams(vmem_limit_bytes=VMEM_LIMIT),
        cost_estimate=pl.CostEstimate(flops=flops, bytes_accessed=8_000_000, transcendentals=0),
        name=name,
    )


def slice_fields(shifts, fractions, z):
    return [shifts[axis, z] for axis in range(3)] + [
        fractions[axis, z].astype(f32) for axis in range(3)
    ]


def place_of_shard(me, shard, members):
    apart = me ^ shard
    quarter = members // PEERS
    peer = apart & (PEERS - 1)
    block = sum(jnp.where(peer == k, c, 0) for c, k in enumerate(ORDER))
    return block * quarter + mirrored(apart // PEERS, quarter)


def build_copy(share, rows, cols):
    def kernel(template, mine):
        mine[...] = template[...]

    return pl.pallas_call(
        kernel,
        out_shape=jax.ShapeDtypeStruct((share, rows, cols), bf16),
        in_specs=vmem_specs(1),
        out_specs=vmem_specs(1)[0],
        compiler_params=pltpu.CompilerParams(vmem_limit_bytes=VMEM_LIMIT),
        cost_estimate=pl.CostEstimate(flops=1_000, bytes_accessed=50_000, transcendentals=0),
        name="own_share",
    )


def build_pack(depth, rows, cols):
    def kernel(shifts, fractions, subjects, near, far, whole, parts, done):
        odd = lax.axis_index("gz") % 2 == 1
        copies = []
        for end, start in enumerate((0, depth - EDGE)):
            at = pl.ds(start, EDGE)
            copies.append(pltpu.make_async_copy(shifts.at[:, at], whole.at[end], done.at[3 * end]))
            copies.append(
                pltpu.make_async_copy(fractions.at[:, at], parts.at[end, 0:3], done.at[3 * end + 1])
            )
            copies.append(
                pltpu.make_async_copy(subjects.at[at], parts.at[end, 3], done.at[3 * end + 2])
            )
        for copy in copies:
            copy.start()
        for copy in copies:
            copy.wait()
        for axis in range(7):
            low, high = [
                (whole[end, axis] if axis < 3 else parts[end, axis - 3]).astype(f32)
                for end in range(2)
            ]
            near[axis] = jnp.where(odd, low, high).astype(bf16)
            far[axis] = jnp.where(odd, high, low).astype(bf16)

    message = jax.ShapeDtypeStruct((7, EDGE, rows, cols), bf16)
    return pl.pallas_call(
        kernel,
        out_shape=[message, message],
        in_specs=[pl.BlockSpec(memory_space=pl.ANY)] * 3,
        out_specs=vmem_specs(2),
        scratch_shapes=[
            pltpu.VMEM((2, 3, EDGE, rows, cols), jnp.int32),
            pltpu.VMEM((2, 4, EDGE, rows, cols), bf16),
            pltpu.SemaphoreType.DMA((6,)),
        ],
        compiler_params=pltpu.CompilerParams(vmem_limit_bytes=62 * 1024 * 1024),
        cost_estimate=pl.CostEstimate(flops=1_000_000, bytes_accessed=2_000_000, transcendentals=0),
        name="pack",
    )


def peer_shard(i, me, share, members, first):
    quarter = members // PEERS
    block = i // share
    return (me ^ (first + block // quarter + PEERS * (block % quarter))) * share + i % share


def end_slices(depth):
    return [*range(SHIFT), *range(depth - SHIFT - 1, depth)]


def build_inner_warp(depth, rows, cols, members):
    share = depth // members
    away = depth - depth // PEERS
    front, count = SHIFT, depth + 2 * SHIFT + 2

    def kernel(pieces, shifts, fractions, subjects, sent, send, shifted, slab):
        me = lax.axis_index("subj")
        quarter = members // PEERS
        slab[0:front] = jnp.zeros((front, rows, cols), f32)
        slab[front + depth : count] = jnp.zeros((count - front - depth, rows, cols), f32)
        for k in range(members):
            shard = me ^ (ORDER[k // quarter] + PEERS * mirrored(k % quarter, quarter))
            slab[pl.ds(front + shard * share, share)] = pieces[k * share : (k + 1) * share].astype(f32)
        for start in range(0, count, count // 2):
            move_columns(slab, shifted, start, count // 2)

        def body(i, carry):
            z = peer_shard(i, me, share, members, 1)
            out = warp_slice(shifted, front + z - SHIFT, *slice_fields(shifts, fractions, z))
            sent[i] = out
            send[i] = subjects[z].astype(f32) - out
            return carry

        lax.fori_loop(0, away, body, 0, unroll=6)

    part = (away, rows, cols)
    return local_call(
        kernel, "inner_warp", [part, part, (TAPS, count, rows, cols)], 4,
        [(count, rows, cols)], 1_000_000_000,
    )


def build_end_warp(depth, rows, cols, members, groups):
    share = depth // members
    quarter, kept = members // PEERS, depth // PEERS
    away = depth - kept
    inner = SHIFT + EDGE
    planes = HALO + inner

    def kernel(
        low_t, high_t, near_t, far_t, shifts, fractions, subjects, send_in, *outs_and_scratch
    ):
        *sends, ends, shifted, slab = outs_and_scratch
        odd = lax.axis_index("gz") % 2 == 1
        me = lax.axis_index("subj")
        inside = has_far(lax.axis_index("gz"), groups)
        near, far = near_t[...].astype(f32), jnp.where(inside, far_t[...].astype(f32), 0.0)
        slab[0:HALO] = jnp.where(odd, near, far)
        slab[HALO:planes] = low_t[0:inner].astype(f32)
        slab[planes : planes + inner] = high_t[HALO - inner : HALO].astype(f32)
        slab[planes + inner : 2 * planes] = jnp.where(odd, far, near)
        move_columns(slab, shifted, 0, 2 * planes)
        for number, send in enumerate(sends):
            send[...] = send_in[number * kept : (number + 1) * kept]
        for number, z in enumerate(end_slices(depth)):
            plane = HALO + z if z < SHIFT else 2 * planes - HALO - depth + z
            out = warp_slice(shifted, plane - SHIFT, *slice_fields(shifts, fractions, z))
            ends[number] = out
            residual = subjects[z].astype(f32) - out
            apart = me ^ (z // share)
            index = (apart // PEERS) * share + z % share
            for k, send in enumerate(sends, 1):

                @pl.when(apart % PEERS == k)
                def _():
                    send[index] = residual

    part = (kept, rows, cols)
    count = len(end_slices(depth))
    return local_call(
        kernel, "end_warp",
        [part] * (PEERS - 1) + [(count, rows, cols), (TAPS, 2 * planes, rows, cols)], 8,
        [(2 * planes, rows, cols)], 300_000_000,
    )


def build_rest_warp(depth, rows, cols, members, groups):
    share = depth // members
    kept = depth // PEERS
    planes = HALO + SHIFT + EDGE

    def kernel(
        moved, moved_ends, sent, ends, near_m, far_m, shifts, fractions, subjects, warped, keep
    ):
        me = lax.axis_index("subj")
        odd = lax.axis_index("gz") % 2 == 1
        inside = has_far(lax.axis_index("gz"), groups)

        def body(i, carry):
            z = peer_shard(i, me, share, members, 0)
            out = warp_slice(moved, z, *slice_fields(shifts, fractions, z))
            warped[EDGE + z] = out
            keep[i] = subjects[z].astype(f32) - out
            for part in range(PEERS - 1):
                number = part * kept + i
                warped[EDGE + peer_shard(number, me, share, members, 1)] = sent[number]
            return carry

        lax.fori_loop(0, kept, body, 0, unroll=4)
        for number, z in enumerate(end_slices(depth)):
            out = ends[number]
            warped[EDGE + z] = out
            apart = me ^ (z // share)

            @pl.when(apart % PEERS == 0)
            def _():
                keep[(apart // PEERS) * share + z % share] = subjects[z].astype(f32) - out

        def outside(z, carry):
            for low in (True, False):
                fields = []
                for axis in range(6):
                    one = near_m[axis, z].astype(f32)
                    two = jnp.where(inside, far_m[axis, z].astype(f32), 0.0)
                    field = jnp.where(odd, one, two) if low else jnp.where(odd, two, one)
                    fields.append(field.astype(jnp.int32) if axis < 3 else field)
                plane = HALO - EDGE + z if low else 2 * planes - HALO + z
                warped[z if low else depth + EDGE + z] = warp_slice(
                    moved_ends, plane - SHIFT, *fields
                )
            return carry

        lax.fori_loop(0, EDGE, outside, 0, unroll=2)

    return local_call(
        kernel, "rest_warp", [(depth + 2 * EDGE, rows, cols), (kept, rows, cols)], 9, [],
        600_000_000,
    )


def band(cols, radius):
    apart = jnp.abs(
        lax.broadcasted_iota(jnp.int32, (cols, cols), 0)
        - lax.broadcasted_iota(jnp.int32, (cols, cols), 1)
    )
    return (apart <= radius).astype(f32)


def column_difference(cols):
    apart = lax.broadcasted_iota(jnp.int32, (cols, cols), 0) - lax.broadcasted_iota(
        jnp.int32, (cols, cols), 1
    )
    return jnp.where(apart == 1, 0.5, jnp.where(apart == -1, -0.5, 0.0)).astype(f32)


def gauss_columns(cols):
    apart = jnp.abs(
        lax.broadcasted_iota(jnp.int32, (cols, cols), 0)
        - lax.broadcasted_iota(jnp.int32, (cols, cols), 1)
    )
    result = jnp.zeros((cols, cols), f32)
    for k, tap in enumerate(GAUSS):
        result = jnp.where(apart == k, f32(tap), result)
    return result


def split(value):
    high = value.astype(bf16)
    return high, (value - high.astype(f32)).astype(bf16)


def take_rows(value, index):
    return jnp.take_along_axis(value, index, axis=0, mode="promise_in_bounds")


def row_window(value, row):
    first = row < WIN
    half = value + take_rows(value, row ^ 1)
    half = half + take_rows(half, row ^ 2)
    outer = jnp.clip(jnp.where(first, row - 1, row + 1), 0, 2 * WIN - 1)
    outer_two = jnp.clip(jnp.where(first, row - 2, row + 2), 0, 2 * WIN - 1)
    reach = jnp.where(first, row, 2 * WIN - 1 - row)
    across = take_rows(value, row ^ WIN) + jnp.where(
        reach >= 1, take_rows(value, outer ^ WIN), 0.0
    )
    return half + across + jnp.where(reach >= 2, take_rows(across, outer_two), 0.0)


def z_windows(load, count):
    x = [load(k) for k in range(count + 2 * WIN)]
    two = [x[k] + x[k + 1] for k in range(count + 2 * WIN - 1)]
    four = [two[k] + two[k + 2] for k in range(count + 2 * WIN - 3)]
    return [four[k] + four[k + 4] + x[k + 8] for k in range(count)]


STEP = 8
CHUNK = 16
PART = 32
SCALE = 1.0 / float((2 * WIN + 1) ** 3)


def flat(value):
    return value.reshape(-1, value.shape[-1])


def square_columns(product, twice):
    pair = jnp.concatenate(split(product), axis=1)
    return jnp.dot(pair, twice, preferred_element_type=f32)


def build_image(depth, rows, cols, groups):
    ext, mid = depth + 2 * EDGE, depth + 2 * SMOOTH

    def kernel(near_m, far_m, subjects, image, mean, variance, boxes):
        odd = lax.axis_index("gz") % 2 == 1
        near = near_m[6].astype(f32)
        far = jnp.where(has_far(lax.axis_index("gz"), groups), far_m[6].astype(f32), 0.0)
        image[0:EDGE] = jnp.where(odd, near, far)
        image[EDGE : EDGE + depth] = subjects[...].astype(f32)
        image[EDGE + depth : ext] = jnp.where(odd, far, near)
        box = band(cols, WIN).astype(bf16)
        twice = jnp.concatenate([box, box], axis=0)

        def columns(i, carry):
            at = pl.ds(i * CHUNK, CHUNK)
            two = flat(image[at])
            results = [
                jnp.dot(two.astype(bf16), box, preferred_element_type=f32),
                square_columns(two * two, twice),
            ]
            for field, result in enumerate(results):
                boxes[field, at] = result.reshape(CHUNK, rows, cols)
            return carry

        lax.fori_loop(0, ext // CHUNK, columns, 0, unroll=True)
        row = lax.broadcasted_iota(jnp.int32, (rows, cols), 0)

        def local(i, carry):
            start = i * STEP
            one, two = [
                [row_window(v, row) * SCALE for v in z_windows(lambda k: boxes[f, start + k], STEP)]
                for f in range(2)
            ]
            for k in range(STEP):
                mean[start + k] = one[k]
                variance[start + k] = two[k] - one[k] * one[k]
            return carry

        lax.fori_loop(0, mid // STEP, local, 0, unroll=True)

    return local_call(
        kernel, "image",
        [(ext, rows, cols), (mid, rows, cols), (mid, rows, cols)], 3,
        [(2, ext, rows, cols)], 400_000_000,
    )


def build_force(depth, rows, cols, groups):
    ext, mid = depth + 2 * EDGE, depth + 2 * SMOOTH

    def kernel(warped, image, mean, variance, force, boxes, slope):
        box = band(cols, WIN)
        first = jnp.concatenate([box, column_difference(cols)], axis=1).astype(bf16)
        box = box.astype(bf16)
        twice = jnp.concatenate([box, box], axis=0)

        def columns(i, carry):
            at = pl.ds(i * CHUNK, CHUNK)
            one, two = flat(warped[at]), flat(image[at])
            both = jnp.dot(one.astype(bf16), first, preferred_element_type=f32)
            results = [both[:, :cols], square_columns(one * one, twice), square_columns(one * two, twice)]
            for field, result in enumerate(results):
                boxes[field, at] = result.reshape(CHUNK, rows, cols)
            slope[at] = both[:, cols:].reshape(CHUNK, rows, cols)
            return carry

        lax.fori_loop(0, ext // CHUNK, columns, 0, unroll=True)
        row = lax.broadcasted_iota(jnp.int32, (rows, cols), 0)

        def local(i, carry):
            start = i * STEP
            means = [
                [row_window(v, row) * SCALE for v in z_windows(lambda k: boxes[f, start + k], STEP)]
                for f in range(3)
            ]
            for k in range(STEP):
                mi, mii, mij = [field[k] for field in means]
                mj, var_j = mean[start + k], variance[start + k]
                at = start + k + WIN
                centre = warped[at]
                var_i = mii - mi * mi
                cov = mij - mi * mj
                factor = (image[at] - mj - cov / (var_i + epsilon) * (centre - mi)) / jnp.sqrt(
                    var_i * var_j + epsilon
                )
                grad_z = 0.5 * (warped[at + 1] - warped[at - 1])
                below = jnp.where(row < rows - 1, pltpu.roll(centre, rows - 1, 0), 0.0)
                above = jnp.where(row > 0, pltpu.roll(centre, 1, 0), 0.0)
                force[0, start + k] = factor * grad_z
                force[1, start + k] = factor * (0.5 * (below - above))
                force[2, start + k] = factor * slope[at]
            return carry

        lax.fori_loop(0, mid // STEP, local, 0, unroll=True)

        @pl.when(lax.axis_index("gz") == 0)
        def _():
            force[:, 0:SMOOTH] = jnp.zeros((3, SMOOTH, rows, cols), f32)

        @pl.when(lax.axis_index("gz") == groups - 1)
        def _():
            force[:, mid - SMOOTH : mid] = jnp.zeros((3, SMOOTH, rows, cols), f32)

    return local_call(
        kernel, "force", [(3, mid, rows, cols)], 4,
        [(3, ext, rows, cols), (ext, rows, cols)], 1_000_000_000,
    )


def build_smooth(depth, rows, cols):
    chunks = depth // PART

    def kernel(force, velocity, padded, result, done):
        g_high, g_low = split(gauss_columns(cols))
        g_all = jnp.concatenate(
            [
                jnp.concatenate([g_high, g_low], axis=1),
                jnp.concatenate([g_high, jnp.zeros_like(g_low)], axis=1),
            ],
            axis=0,
        )
        padded[...] = jnp.zeros(padded.shape, f32)

        def sent(i):
            at = pl.ds(i * PART, PART)
            return pltpu.make_async_copy(result.at[:, at], velocity.at[:, at], done.at[i])

        def finish(i, carry):
            start = i * PART
            for axis in range(3):
                x = [force[axis, start + k] for k in range(PART + 2 * SMOOTH)]
                for k in range(PART):
                    value = GAUSS[0] * x[k + SMOOTH]
                    for d in range(1, SMOOTH + 1):
                        value = value + GAUSS[d] * (x[k + SMOOTH - d] + x[k + SMOOTH + d])
                    padded[axis, k, SMOOTH : SMOOTH + rows] = value
                highs, lows = [], []
                for k in range(0, PART, 2):
                    both = []
                    for n in (k, k + 1):
                        value = GAUSS[0] * padded[axis, n, SMOOTH : SMOOTH + rows]
                        for d in range(1, SMOOTH + 1):
                            value = value + GAUSS[d] * (
                                padded[axis, n, SMOOTH - d : SMOOTH - d + rows]
                                + padded[axis, n, SMOOTH + d : SMOOTH + d + rows]
                            )
                        both.append(value)
                    high, low = split(jnp.concatenate(both, axis=0))
                    highs.append(high)
                    lows.append(low)
                pair = jnp.concatenate(
                    [jnp.concatenate(highs, axis=0), jnp.concatenate(lows, axis=0)], axis=1
                )
                mixed = jnp.dot(pair, g_all, preferred_element_type=f32)
                result[axis, pl.ds(start, PART)] = (mixed[:, :cols] + mixed[:, cols:]).reshape(
                    PART, rows, cols
                )
            sent(i).start()
            return carry

        lax.fori_loop(0, chunks, finish, 0, unroll=True)
        for i in range(chunks):
            sent(i).wait()

    return pl.pallas_call(
        kernel,
        out_shape=[jax.ShapeDtypeStruct((3, depth, rows, cols), f32)],
        in_specs=vmem_specs(1),
        out_specs=[pl.BlockSpec(memory_space=pl.ANY)],
        scratch_shapes=[
            pltpu.VMEM((3, PART, rows + 2 * SMOOTH, cols), f32),
            pltpu.VMEM((3, depth, rows, cols), f32),
            pltpu.SemaphoreType.DMA((chunks,)),
        ],
        compiler_params=pltpu.CompilerParams(vmem_limit_bytes=VMEM_LIMIT),
        cost_estimate=pl.CostEstimate(flops=600_000_000, bytes_accessed=8_000_000, transcendentals=0),
        name="smooth",
    )


def per_device(template, subjects, shifts, fractions):
    groups = lax.axis_size("gz")
    members = lax.axis_size("subj")
    subject_count, depth, rows, cols = subjects.shape
    share = depth // members
    reach = -(-HALO // share)
    me = lax.axis_index("subj")
    bits = bits_of(members)[2:]
    subject, shift, fraction = subjects[0], shifts[0], fractions[0]

    arrived = swap(template, "subj", bits[-1])
    mine = build_copy(share, rows, cols)(template)
    to_near, to_far = build_pack(depth, rows, cols)(shift, fraction, subject)
    pieces = jnp.concatenate([mine, arrived], axis=0)
    pieces, to_near, to_far = lax.optimization_barrier((pieces, to_near, to_far))
    near_m, far_m = swap_near(to_near, "gz"), swap_far(to_far, "gz")
    for bit in bits[-2::-1]:
        pieces = jnp.concatenate([pieces, swap(pieces, "subj", bit)], axis=0)
    pieces = jnp.concatenate(
        [pieces] + [swap(pieces, "subj", k) for k in ORDER[1:]], axis=0
    )

    def shares(numbers):
        starts = [place_of_shard(me, number, members) * share for number in numbers]
        return jnp.concatenate(
            [lax.dynamic_slice_in_dim(pieces, start, share, 0) for start in starts], axis=0
        )

    low_t = shares(range(reach))[:HALO]
    high_t = shares(range(members - reach, members))[-HALO:]
    to_near, to_far = at_ends("gz", low_t, high_t)
    near_t, far_t = swap_near(to_near, "gz"), swap_far(to_far, "gz")

    sent, send, moved = build_inner_warp(depth, rows, cols, members)(pieces, shift, fraction, subject)
    *sends, ends, moved_ends = build_end_warp(depth, rows, cols, members, groups)(
        low_t, high_t, near_t, far_t, shift, fraction, subject, send
    )

    parts = [swap(sends[k - 1], "subj", k) for k in (3, 1, 2)]
    warped, keep = build_rest_warp(depth, rows, cols, members, groups)(
        moved, moved_ends, sent, ends, near_m, far_m, shift, fraction, subject
    )
    near_m, far_m, subject, warped = lax.optimization_barrier((near_m, far_m, subject, warped))
    image, mean, variance = build_image(depth, rows, cols, groups)(near_m, far_m, subject)
    (force,) = build_force(depth, rows, cols, groups)(warped, image, mean, variance)
    *parts, force = lax.optimization_barrier((*parts, force))
    keep = keep + parts[0] + parts[1] + parts[2]
    for bit in bits:
        pairs = keep.reshape((-1, 2, share) + keep.shape[1:])
        keep, send = [pairs[:, part].reshape((-1,) + keep.shape[1:]) for part in (0, 1)]
        keep = keep + swap(send, "subj", bit)
    (velocity,) = build_smooth(depth, rows, cols)(force)
    template_force = keep * (1.0 / math.sqrt(subject_count * members))
    return (velocity[None], template_force)


def solution(mesh):
    placed = (
        P(("gz", "subj"), None, None),
        P("subj", "gz", None, None),
        P("subj", None, "gz", None, None),
        P("subj", None, "gz", None, None),
    )
    return jax.shard_map(
        per_device,
        mesh=mesh,
        in_specs=placed,
        out_specs=(P("subj", None, "gz", None, None), P(("gz", "subj"), None, None)),
        check_vma=False,
    )
```

```python
import math

import jax
import jax.numpy as jnp
from jax import lax
from jax.experimental import pallas as pl
from jax.experimental.pallas import tpu as pltpu
from jax.sharding import PartitionSpec as P

SHIFT = 2
WIN = 4
SMOOTH = 4
EDGE = WIN + SMOOTH
HALO = EDGE + SHIFT + 1
TAPS = 2 * SHIFT + 2
sigma = 1.5
epsilon = 1e-05
f32 = jnp.float32
bf16 = jnp.bfloat16
PEERS = 4
ORDER = (0, 1, 3, 2)
VMEM_LIMIT = 48 * 1024 * 1024

raw = [math.exp(-k * k / (2 * sigma * sigma)) for k in range(SMOOTH + 1)]
norm = raw[0] + 2 * sum(raw[1:])
GAUSS = [value / norm for value in raw]


def swap(block, axis, bit):
    count = lax.axis_size(axis)
    return lax.ppermute(block, axis, [(i, i ^ bit) for i in range(count)])


def swap_near(block, axis):
    count = lax.axis_size(axis)
    pairs = [(i, i ^ 1) for i in range(count) if (i ^ 1) < count]
    return lax.ppermute(block, axis, pairs)


def swap_far(block, axis):
    count = lax.axis_size(axis)
    assert count % 2 == 0
    return lax.ppermute(
        block, axis, [(i, (i + 1 if i % 2 else i - 1) % count) for i in range(count)]
    )


def has_far(group, groups):
    return (group != 0) & (group != groups - 1)


def bits_of(count):
    return [1 << place for place in range(count.bit_length() - 1)]


def mirrored(number, count):
    places = count.bit_length() - 1
    return sum(((number >> place) & 1) << (places - 1 - place) for place in range(places))


def at_ends(axis, low, high):
    odd = lax.axis_index(axis) % 2 == 1
    return jnp.where(odd, low, high), jnp.where(odd, high, low)


def shift_matrix(offsets, cols):
    source = lax.broadcasted_iota(jnp.int32, (cols, cols), 0)
    target = lax.broadcasted_iota(jnp.int32, (cols, cols), 1)
    return jnp.concatenate(
        [(source == target + offset).astype(f32) for offset in offsets], axis=1
    ).astype(bf16)


def rows_at(value, index):
    return jnp.take_along_axis(value, index, axis=0, mode="promise_in_bounds")


def even_odd(base, frac):
    even = (base & 1) == 0
    rest = 1.0 - frac
    return jnp.where(even, rest, frac), jnp.where(even, frac, rest)


def warp_slice(shifted, plane, sz, sr, sc, fz, fr, fc):
    rows = sz.shape[0]
    row = lax.broadcasted_iota(jnp.int32, sz.shape, 0) + sr
    after = row + 1
    index0, index1 = row & (rows - 1), after & (rows - 1)
    weight0 = jnp.where(index0 == row, 1.0 - fr, 0.0)
    weight1 = jnp.where(index1 == after, fr, 0.0)
    col_e, col_o = even_odd(sc, fc)
    dep_e, dep_o = even_odd(sz, fz)
    picks = {k: (sc >= k - 3, sz >= k - 3) for k in range(2, TAPS)}
    planes = [None, None]
    for kz in range(TAPS):
        corner = [[None, None], [None, None]]
        for kc in range(TAPS):
            value = shifted[kc, plane + kz]
            for b, index in ((0, index0), (1, index1)):
                taken = rows_at(value, index)
                if kc < 2:
                    corner[b][kc] = taken
                else:
                    corner[b][kc % 2] = jnp.where(picks[kc][0], taken, corner[b][kc % 2])
        flat = corner[0] + corner[1]
        if kz < 2:
            planes[kz] = flat
        else:
            mask = picks[kz][1]
            planes[kz % 2] = [jnp.where(mask, new, old) for new, old in zip(flat, planes[kz % 2])]
    parts = []
    for e0, o0, e1, o1 in planes:
        parts.append(
            weight0 * (col_e * e0 + col_o * o0) + weight1 * (col_e * e1 + col_o * o1)
        )
    summed = dep_e * parts[0] + dep_o * parts[1]
    return summed.astype(bf16).astype(f32)


def move_columns(slab, shifted, start, step):
    rows, cols = slab.shape[1:]
    offsets = [k - SHIFT for k in range(TAPS) if k != SHIFT]
    matrix = shift_matrix(offsets, cols)
    block = slab[start : start + step]
    shifted[SHIFT, start : start + step] = block
    moved = jnp.dot(
        block.reshape(step * rows, cols).astype(bf16), matrix, preferred_element_type=f32
    )
    for number, offset in enumerate(offsets):
        shifted[offset + SHIFT, start : start + step] = moved[
            :, number * cols : (number + 1) * cols
        ].reshape(step, rows, cols)


def vmem_specs(count):
    return [pl.BlockSpec(memory_space=pltpu.VMEM)] * count


def local_call(kernel, name, outs, inputs, scratch, flops):
    return pl.pallas_call(
        kernel,
        out_shape=[jax.ShapeDtypeStruct(shape, f32) for shape in outs],
        in_specs=vmem_specs(inputs),
        out_specs=vmem_specs(len(outs)),
        scratch_shapes=[pltpu.VMEM(shape, f32) for shape in scratch],
        compiler_params=pltpu.CompilerParams(vmem_limit_bytes=VMEM_LIMIT),
        cost_estimate=pl.CostEstimate(flops=flops, bytes_accessed=8_000_000, transcendentals=0),
        name=name,
    )


def slice_fields(shifts, fractions, z):
    return [shifts[axis, z] for axis in range(3)] + [
        fractions[axis, z].astype(f32) for axis in range(3)
    ]


def place_of_shard(me, shard, members):
    apart = me ^ shard
    quarter = members // PEERS
    peer = apart & (PEERS - 1)
    block = sum(jnp.where(peer == k, c, 0) for c, k in enumerate(ORDER))
    return block * quarter + mirrored(apart // PEERS, quarter)


def build_copy(share, rows, cols):
    def kernel(template, mine):
        mine[...] = template[...]

    return pl.pallas_call(
        kernel,
        out_shape=jax.ShapeDtypeStruct((share, rows, cols), bf16),
        in_specs=vmem_specs(1),
        out_specs=vmem_specs(1)[0],
        compiler_params=pltpu.CompilerParams(vmem_limit_bytes=VMEM_LIMIT),
        cost_estimate=pl.CostEstimate(flops=1_000, bytes_accessed=50_000, transcendentals=0),
        name="own_share",
    )


def build_pack(depth, rows, cols):
    def kernel(shifts, fractions, subjects, near, far, whole, parts, done):
        odd = lax.axis_index("gz") % 2 == 1
        copies = []
        for end, start in enumerate((0, depth - EDGE)):
            at = pl.ds(start, EDGE)
            copies.append(pltpu.make_async_copy(shifts.at[:, at], whole.at[end], done.at[3 * end]))
            copies.append(
                pltpu.make_async_copy(fractions.at[:, at], parts.at[end, 0:3], done.at[3 * end + 1])
            )
            copies.append(
                pltpu.make_async_copy(subjects.at[at], parts.at[end, 3], done.at[3 * end + 2])
            )
        for copy in copies:
            copy.start()
        for copy in copies:
            copy.wait()
        for axis in range(7):
            low, high = [
                (whole[end, axis] if axis < 3 else parts[end, axis - 3]).astype(f32)
                for end in range(2)
            ]
            near[axis] = jnp.where(odd, low, high).astype(bf16)
            far[axis] = jnp.where(odd, high, low).astype(bf16)

    message = jax.ShapeDtypeStruct((7, EDGE, rows, cols), bf16)
    return pl.pallas_call(
        kernel,
        out_shape=[message, message],
        in_specs=[pl.BlockSpec(memory_space=pl.ANY)] * 3,
        out_specs=vmem_specs(2),
        scratch_shapes=[
            pltpu.VMEM((2, 3, EDGE, rows, cols), jnp.int32),
            pltpu.VMEM((2, 4, EDGE, rows, cols), bf16),
            pltpu.SemaphoreType.DMA((6,)),
        ],
        compiler_params=pltpu.CompilerParams(vmem_limit_bytes=62 * 1024 * 1024),
        cost_estimate=pl.CostEstimate(flops=1_000_000, bytes_accessed=2_000_000, transcendentals=0),
        name="pack",
    )


def peer_shard(i, me, share, members, first):
    quarter = members // PEERS
    block = i // share
    return (me ^ (first + block // quarter + PEERS * (block % quarter))) * share + i % share


def end_slices(depth):
    return [*range(SHIFT), *range(depth - SHIFT - 1, depth)]


def build_inner_warp(depth, rows, cols, members):
    share = depth // members
    away = depth - depth // PEERS
    front, count = SHIFT, depth + 2 * SHIFT + 2

    def kernel(pieces, shifts, fractions, subjects, sent, send, shifted, slab):
        me = lax.axis_index("subj")
        quarter = members // PEERS
        slab[0:front] = jnp.zeros((front, rows, cols), f32)
        slab[front + depth : count] = jnp.zeros((count - front - depth, rows, cols), f32)
        for k in range(members):
            shard = me ^ (ORDER[k // quarter] + PEERS * mirrored(k % quarter, quarter))
            slab[pl.ds(front + shard * share, share)] = pieces[k * share : (k + 1) * share].astype(f32)
        for start in range(0, count, count // 2):
            move_columns(slab, shifted, start, count // 2)

        def body(i, carry):
            z = peer_shard(i, me, share, members, 1)
            out = warp_slice(shifted, front + z - SHIFT, *slice_fields(shifts, fractions, z))
            sent[i] = out
            send[i] = subjects[z].astype(f32) - out
            return carry

        lax.fori_loop(0, away, body, 0, unroll=8)

    part = (away, rows, cols)
    return local_call(
        kernel, "inner_warp", [part, part, (TAPS, count, rows, cols)], 4,
        [(count, rows, cols)], 1_000_000_000,
    )


def end_planes():
    return 3 * SHIFT + 1, 3 * SHIFT + 2


def build_end_warp(depth, rows, cols, members, groups):
    share = depth // members
    kept = depth // PEERS
    below, above = end_planes()
    planes = below + above

    def kernel(low_t, high_t, near_t, far_t, shifts, fractions, subjects, send_in, *outs_and_scratch):
        *sends, ends, slab, shifted = outs_and_scratch
        odd = lax.axis_index("gz") % 2 == 1
        me = lax.axis_index("subj")
        inside = has_far(lax.axis_index("gz"), groups)
        near, far = near_t[...].astype(f32), jnp.where(inside, far_t[...].astype(f32), 0.0)
        front, back = below - SHIFT, above - SHIFT - 1
        slab[0:SHIFT] = jnp.where(odd, near, far)[HALO - SHIFT :]
        slab[SHIFT:below] = low_t[0:front].astype(f32)
        slab[below : below + back] = high_t[HALO - back : HALO].astype(f32)
        slab[below + back : planes] = jnp.where(odd, far, near)[: SHIFT + 1]
        move_columns(slab, shifted, 0, planes)
        for number, send in enumerate(sends):
            send[...] = send_in[number * kept : (number + 1) * kept]
        for number, z in enumerate(end_slices(depth)):
            plane = z if z < SHIFT else below + z - (depth - SHIFT - 1)
            out = warp_slice(shifted, plane, *slice_fields(shifts, fractions, z))
            ends[number] = out
            residual = subjects[z].astype(f32) - out
            apart = me ^ (z // share)
            index = (apart // PEERS) * share + z % share
            for k, send in enumerate(sends, 1):

                @pl.when(apart % PEERS == k)
                def _():
                    send[index] = residual

    part = (kept, rows, cols)
    count = len(end_slices(depth))
    return local_call(
        kernel, "end_warp", [part] * (PEERS - 1) + [(count, rows, cols)], 8,
        [(planes, rows, cols), (TAPS, planes, rows, cols)], 300_000_000,
    )


def build_rest_warp(depth, rows, cols, members, groups):
    share = depth // members
    kept = depth // PEERS
    planes = HALO + SHIFT + EDGE

    def kernel(
        moved, low_t, high_t, near_t, far_t, sent, ends, near_m, far_m, shifts, fractions, subjects,
        warped, keep, slab, moved_ends,
    ):
        me = lax.axis_index("subj")
        odd = lax.axis_index("gz") % 2 == 1
        inside = has_far(lax.axis_index("gz"), groups)
        inner = SHIFT + EDGE
        near, far = near_t[...].astype(f32), jnp.where(inside, far_t[...].astype(f32), 0.0)
        slab[0:HALO] = jnp.where(odd, near, far)
        slab[HALO:planes] = low_t[0:inner].astype(f32)
        slab[planes : planes + inner] = high_t[HALO - inner : HALO].astype(f32)
        slab[planes + inner : 2 * planes] = jnp.where(odd, far, near)
        move_columns(slab, moved_ends, 0, 2 * planes)

        def body(i, carry):
            z = peer_shard(i, me, share, members, 0)
            out = warp_slice(moved, z, *slice_fields(shifts, fractions, z))
            warped[EDGE + z] = out
            keep[i] = subjects[z].astype(f32) - out
            for part in range(PEERS - 1):
                number = part * kept + i
                warped[EDGE + peer_shard(number, me, share, members, 1)] = sent[number]
            return carry

        lax.fori_loop(0, kept, body, 0, unroll=4)
        for number, z in enumerate(end_slices(depth)):
            out = ends[number]
            warped[EDGE + z] = out
            apart = me ^ (z // share)

            @pl.when(apart % PEERS == 0)
            def _():
                keep[(apart // PEERS) * share + z % share] = subjects[z].astype(f32) - out

        def outside(z, carry):
            for low in (True, False):
                fields = []
                for axis in range(6):
                    one = near_m[axis, z].astype(f32)
                    two = jnp.where(inside, far_m[axis, z].astype(f32), 0.0)
                    field = jnp.where(odd, one, two) if low else jnp.where(odd, two, one)
                    fields.append(field.astype(jnp.int32) if axis < 3 else field)
                plane = HALO - EDGE + z if low else 2 * planes - HALO + z
                warped[z if low else depth + EDGE + z] = warp_slice(
                    moved_ends, plane - SHIFT, *fields
                )
            return carry

        lax.fori_loop(0, EDGE, outside, 0, unroll=2)

    return local_call(
        kernel, "rest_warp", [(depth + 2 * EDGE, rows, cols), (kept, rows, cols)], 12,
        [(2 * planes, rows, cols), (TAPS, 2 * planes, rows, cols)],
        600_000_000,
    )


def band(cols, radius):
    apart = jnp.abs(
        lax.broadcasted_iota(jnp.int32, (cols, cols), 0)
        - lax.broadcasted_iota(jnp.int32, (cols, cols), 1)
    )
    return (apart <= radius).astype(f32)


def column_difference(cols):
    apart = lax.broadcasted_iota(jnp.int32, (cols, cols), 0) - lax.broadcasted_iota(
        jnp.int32, (cols, cols), 1
    )
    return jnp.where(apart == 1, 0.5, jnp.where(apart == -1, -0.5, 0.0)).astype(f32)


def gauss_columns(cols):
    apart = jnp.abs(
        lax.broadcasted_iota(jnp.int32, (cols, cols), 0)
        - lax.broadcasted_iota(jnp.int32, (cols, cols), 1)
    )
    result = jnp.zeros((cols, cols), f32)
    for k, tap in enumerate(GAUSS):
        result = jnp.where(apart == k, f32(tap), result)
    return result


def split(value):
    high = value.astype(bf16)
    return high, (value - high.astype(f32)).astype(bf16)


def take_rows(value, index):
    return jnp.take_along_axis(value, index, axis=0, mode="promise_in_bounds")


def row_window(value, row):
    first = row < WIN
    half = value + take_rows(value, row ^ 1)
    half = half + take_rows(half, row ^ 2)
    outer = jnp.clip(jnp.where(first, row - 1, row + 1), 0, 2 * WIN - 1)
    outer_two = jnp.clip(jnp.where(first, row - 2, row + 2), 0, 2 * WIN - 1)
    reach = jnp.where(first, row, 2 * WIN - 1 - row)
    across = take_rows(value, row ^ WIN) + jnp.where(
        reach >= 1, take_rows(value, outer ^ WIN), 0.0
    )
    return half + across + jnp.where(reach >= 2, take_rows(across, outer_two), 0.0)


def z_windows(load, count):
    x = [load(k) for k in range(count + 2 * WIN)]
    two = [x[k] + x[k + 1] for k in range(count + 2 * WIN - 1)]
    four = [two[k] + two[k + 2] for k in range(count + 2 * WIN - 3)]
    return [four[k] + four[k + 4] + x[k + 8] for k in range(count)]


STEP = 8
CHUNK = 16
PART = 32
SCALE = 1.0 / float((2 * WIN + 1) ** 3)


def flat(value):
    return value.reshape(-1, value.shape[-1])


def square_columns(product, twice):
    pair = jnp.concatenate(split(product), axis=1)
    return jnp.dot(pair, twice, preferred_element_type=f32)


def build_image(depth, rows, cols, groups):
    ext, mid = depth + 2 * EDGE, depth + 2 * SMOOTH

    def kernel(near_m, far_m, subjects, image, mean, variance, boxes):
        odd = lax.axis_index("gz") % 2 == 1
        near = near_m[6].astype(f32)
        far = jnp.where(has_far(lax.axis_index("gz"), groups), far_m[6].astype(f32), 0.0)
        image[0:EDGE] = jnp.where(odd, near, far)
        image[EDGE : EDGE + depth] = subjects[...].astype(f32)
        image[EDGE + depth : ext] = jnp.where(odd, far, near)
        box = band(cols, WIN).astype(bf16)
        twice = jnp.concatenate([box, box], axis=0)

        def columns(i, carry):
            at = pl.ds(i * CHUNK, CHUNK)
            two = flat(image[at])
            results = [
                jnp.dot(two.astype(bf16), box, preferred_element_type=f32),
                square_columns(two * two, twice),
            ]
            for field, result in enumerate(results):
                boxes[field, at] = result.reshape(CHUNK, rows, cols)
            return carry

        lax.fori_loop(0, ext // CHUNK, columns, 0, unroll=True)
        row = lax.broadcasted_iota(jnp.int32, (rows, cols), 0)

        def local(i, carry):
            start = i * STEP
            one, two = [
                [row_window(v, row) * SCALE for v in z_windows(lambda k: boxes[f, start + k], STEP)]
                for f in range(2)
            ]
            for k in range(STEP):
                mean[start + k] = one[k]
                variance[start + k] = two[k] - one[k] * one[k]
            return carry

        lax.fori_loop(0, mid // STEP, local, 0, unroll=True)

    return local_call(
        kernel, "image",
        [(ext, rows, cols), (mid, rows, cols), (mid, rows, cols)], 3,
        [(2, ext, rows, cols)], 400_000_000,
    )


def build_force(depth, rows, cols, groups):
    ext, mid = depth + 2 * EDGE, depth + 2 * SMOOTH

    def kernel(warped, image, mean, variance, force, boxes, slope):
        box = band(cols, WIN)
        first = jnp.concatenate([box, column_difference(cols)], axis=1).astype(bf16)
        box = box.astype(bf16)
        twice = jnp.concatenate([box, box], axis=0)

        def columns(i, carry):
            at = pl.ds(i * CHUNK, CHUNK)
            one, two = flat(warped[at]), flat(image[at])
            both = jnp.dot(one.astype(bf16), first, preferred_element_type=f32)
            results = [both[:, :cols], square_columns(one * one, twice), square_columns(one * two, twice)]
            for field, result in enumerate(results):
                boxes[field, at] = result.reshape(CHUNK, rows, cols)
            slope[at] = both[:, cols:].reshape(CHUNK, rows, cols)
            return carry

        lax.fori_loop(0, ext // CHUNK, columns, 0, unroll=True)
        row = lax.broadcasted_iota(jnp.int32, (rows, cols), 0)

        def local(i, carry):
            start = i * STEP
            means = [
                [row_window(v, row) * SCALE for v in z_windows(lambda k: boxes[f, start + k], STEP)]
                for f in range(3)
            ]
            for k in range(STEP):
                mi, mii, mij = [field[k] for field in means]
                mj, var_j = mean[start + k], variance[start + k]
                at = start + k + WIN
                centre = warped[at]
                var_i = mii - mi * mi
                cov = mij - mi * mj
                factor = (image[at] - mj - cov / (var_i + epsilon) * (centre - mi)) / jnp.sqrt(
                    var_i * var_j + epsilon
                )
                grad_z = 0.5 * (warped[at + 1] - warped[at - 1])
                below = jnp.where(row < rows - 1, pltpu.roll(centre, rows - 1, 0), 0.0)
                above = jnp.where(row > 0, pltpu.roll(centre, 1, 0), 0.0)
                force[0, start + k] = factor * grad_z
                force[1, start + k] = factor * (0.5 * (below - above))
                force[2, start + k] = factor * slope[at]
            return carry

        lax.fori_loop(0, mid // STEP, local, 0, unroll=True)

        @pl.when(lax.axis_index("gz") == 0)
        def _():
            force[:, 0:SMOOTH] = jnp.zeros((3, SMOOTH, rows, cols), f32)

        @pl.when(lax.axis_index("gz") == groups - 1)
        def _():
            force[:, mid - SMOOTH : mid] = jnp.zeros((3, SMOOTH, rows, cols), f32)

    return local_call(
        kernel, "force", [(3, mid, rows, cols)], 4,
        [(3, ext, rows, cols), (ext, rows, cols)], 1_000_000_000,
    )


def build_smooth(depth, rows, cols):
    chunks = depth // PART

    def kernel(force, velocity, padded, result, done):
        g_high, g_low = split(gauss_columns(cols))
        g_all = jnp.concatenate(
            [
                jnp.concatenate([g_high, g_low], axis=1),
                jnp.concatenate([g_high, jnp.zeros_like(g_low)], axis=1),
            ],
            axis=0,
        )
        padded[...] = jnp.zeros(padded.shape, f32)

        def sent(i):
            at = pl.ds(i * PART, PART)
            return pltpu.make_async_copy(result.at[:, at], velocity.at[:, at], done.at[i])

        def finish(i, carry):
            start = i * PART
            for axis in range(3):
                x = [force[axis, start + k] for k in range(PART + 2 * SMOOTH)]
                for k in range(PART):
                    value = GAUSS[0] * x[k + SMOOTH]
                    for d in range(1, SMOOTH + 1):
                        value = value + GAUSS[d] * (x[k + SMOOTH - d] + x[k + SMOOTH + d])
                    padded[axis, k, SMOOTH : SMOOTH + rows] = value
                highs, lows = [], []
                for k in range(0, PART, 2):
                    both = []
                    for n in (k, k + 1):
                        value = GAUSS[0] * padded[axis, n, SMOOTH : SMOOTH + rows]
                        for d in range(1, SMOOTH + 1):
                            value = value + GAUSS[d] * (
                                padded[axis, n, SMOOTH - d : SMOOTH - d + rows]
                                + padded[axis, n, SMOOTH + d : SMOOTH + d + rows]
                            )
                        both.append(value)
                    high, low = split(jnp.concatenate(both, axis=0))
                    highs.append(high)
                    lows.append(low)
                pair = jnp.concatenate(
                    [jnp.concatenate(highs, axis=0), jnp.concatenate(lows, axis=0)], axis=1
                )
                mixed = jnp.dot(pair, g_all, preferred_element_type=f32)
                result[axis, pl.ds(start, PART)] = (mixed[:, :cols] + mixed[:, cols:]).reshape(
                    PART, rows, cols
                )
            sent(i).start()
            return carry

        lax.fori_loop(0, chunks, finish, 0, unroll=True)
        for i in range(chunks):
            sent(i).wait()

    return pl.pallas_call(
        kernel,
        out_shape=[jax.ShapeDtypeStruct((3, depth, rows, cols), f32)],
        in_specs=vmem_specs(1),
        out_specs=[pl.BlockSpec(memory_space=pl.ANY)],
        scratch_shapes=[
            pltpu.VMEM((3, PART, rows + 2 * SMOOTH, cols), f32),
            pltpu.VMEM((3, depth, rows, cols), f32),
            pltpu.SemaphoreType.DMA((chunks,)),
        ],
        compiler_params=pltpu.CompilerParams(vmem_limit_bytes=VMEM_LIMIT),
        cost_estimate=pl.CostEstimate(flops=600_000_000, bytes_accessed=8_000_000, transcendentals=0),
        name="smooth",
    )


def per_device(template, subjects, shifts, fractions):
    groups = lax.axis_size("gz")
    members = lax.axis_size("subj")
    subject_count, depth, rows, cols = subjects.shape
    share = depth // members
    reach = -(-HALO // share)
    me = lax.axis_index("subj")
    bits = bits_of(members)[2:]
    subject, shift, fraction = subjects[0], shifts[0], fractions[0]

    arrived = swap(template, "subj", bits[-1])
    mine = build_copy(share, rows, cols)(template)
    to_near, to_far = build_pack(depth, rows, cols)(shift, fraction, subject)
    pieces = jnp.concatenate([mine, arrived], axis=0)
    pieces, to_near, to_far = lax.optimization_barrier((pieces, to_near, to_far))
    near_m, far_m = swap_near(to_near, "gz"), swap_far(to_far, "gz")
    for bit in bits[-2::-1]:
        pieces = jnp.concatenate([pieces, swap(pieces, "subj", bit)], axis=0)
    pieces = jnp.concatenate(
        [pieces] + [swap(pieces, "subj", k) for k in ORDER[1:]], axis=0
    )

    def shares(numbers):
        starts = [place_of_shard(me, number, members) * share for number in numbers]
        return jnp.concatenate(
            [lax.dynamic_slice_in_dim(pieces, start, share, 0) for start in starts], axis=0
        )

    low_t = shares(range(reach))[:HALO]
    high_t = shares(range(members - reach, members))[-HALO:]
    to_near, to_far = at_ends("gz", low_t, high_t)
    near_t, far_t = swap_near(to_near, "gz"), swap_far(to_far, "gz")

    sent, send, moved = build_inner_warp(depth, rows, cols, members)(pieces, shift, fraction, subject)
    *sends, ends = build_end_warp(depth, rows, cols, members, groups)(
        low_t, high_t, near_t, far_t, shift, fraction, subject, send
    )

    parts = [swap(sends[k - 1], "subj", k) for k in (3, 1, 2)]
    warped, keep = build_rest_warp(depth, rows, cols, members, groups)(
        moved, low_t, high_t, near_t, far_t, sent, ends, near_m, far_m, shift, fraction, subject
    )
    near_m, far_m, subject, warped = lax.optimization_barrier((near_m, far_m, subject, warped))
    image, mean, variance = build_image(depth, rows, cols, groups)(near_m, far_m, subject)
    (force,) = build_force(depth, rows, cols, groups)(warped, image, mean, variance)
    *parts, force = lax.optimization_barrier((*parts, force))
    keep = keep + parts[0] + parts[1] + parts[2]
    for bit in bits:
        pairs = keep.reshape((-1, 2, share) + keep.shape[1:])
        keep, send = [pairs[:, part].reshape((-1,) + keep.shape[1:]) for part in (0, 1)]
        arrived = swap(send, "subj", bit)
        if bit != bits[-1]:
            keep = keep + arrived
    (velocity,) = build_smooth(depth, rows, cols)(force)
    scale = 1.0 / math.sqrt(subject_count * members)

    def finish(one, two, out):
        out[...] = (one[...] + two[...]) * scale

    (template_force,) = local_call(finish, "finish", [(share, rows, cols)], 2, [], 10_000)(keep, arrived)
    return (velocity[None], template_force)


def solution(mesh):
    placed = (
        P(("gz", "subj"), None, None),
        P("subj", "gz", None, None),
        P("subj", None, "gz", None, None),
        P("subj", None, "gz", None, None),
    )
    return jax.shard_map(
        per_device,
        mesh=mesh,
        in_specs=placed,
        out_specs=(P("subj", None, "gz", None, None), P(("gz", "subj"), None, None)),
        check_vma=False,
    )
```

```python
import math

import jax
import jax.numpy as jnp
from jax import lax
from jax.experimental import pallas as pl
from jax.experimental.pallas import tpu as pltpu
from jax.sharding import PartitionSpec as P

SHIFT = 2
WIN = 4
SMOOTH = 4
EDGE = WIN + SMOOTH
HALO = EDGE + SHIFT + 1
TAPS = 2 * SHIFT + 2
sigma = 1.5
epsilon = 1e-05
f32 = jnp.float32
bf16 = jnp.bfloat16
PEERS = 4
ORDER = (0, 3, 1, 2)
VMEM_LIMIT = 48 * 1024 * 1024

raw = [math.exp(-k * k / (2 * sigma * sigma)) for k in range(SMOOTH + 1)]
norm = raw[0] + 2 * sum(raw[1:])
GAUSS = [value / norm for value in raw]


def swap(block, axis, bit):
    count = lax.axis_size(axis)
    return lax.ppermute(block, axis, [(i, i ^ bit) for i in range(count)])


def swap_near(block, axis):
    count = lax.axis_size(axis)
    pairs = [(i, i ^ 1) for i in range(count) if (i ^ 1) < count]
    return lax.ppermute(block, axis, pairs)


def swap_far(block, axis):
    count = lax.axis_size(axis)
    assert count % 2 == 0
    return lax.ppermute(
        block, axis, [(i, (i + 1 if i % 2 else i - 1) % count) for i in range(count)]
    )


def has_far(group, groups):
    return (group != 0) & (group != groups - 1)


def bits_of(count):
    return [1 << place for place in range(count.bit_length() - 1)]


def mirrored(number, count):
    places = count.bit_length() - 1
    return sum(((number >> place) & 1) << (places - 1 - place) for place in range(places))


def at_ends(axis, low, high):
    odd = lax.axis_index(axis) % 2 == 1
    return jnp.where(odd, low, high), jnp.where(odd, high, low)


def shift_matrix(offsets, cols):
    source = lax.broadcasted_iota(jnp.int32, (cols, cols), 0)
    target = lax.broadcasted_iota(jnp.int32, (cols, cols), 1)
    return jnp.concatenate(
        [(source == target + offset).astype(f32) for offset in offsets], axis=1
    ).astype(bf16)


def rows_at(value, index):
    return jnp.take_along_axis(value, index, axis=0, mode="promise_in_bounds")


def even_odd(base, frac):
    even = (base & 1) == 0
    rest = 1.0 - frac
    return jnp.where(even, rest, frac), jnp.where(even, frac, rest)


def warp_slice(shifted, plane, sz, sr, sc, fz, fr, fc):
    rows = sz.shape[0]
    row = lax.broadcasted_iota(jnp.int32, sz.shape, 0) + sr
    after = row + 1
    index0, index1 = row & (rows - 1), after & (rows - 1)
    weight0 = jnp.where(index0 == row, 1.0 - fr, 0.0)
    weight1 = jnp.where(index1 == after, fr, 0.0)
    col_e, col_o = even_odd(sc, fc)
    dep_e, dep_o = even_odd(sz, fz)
    picks = {k: (sc >= k - 3, sz >= k - 3) for k in range(2, TAPS)}
    planes = [None, None]
    for kz in range(TAPS):
        corner = [[None, None], [None, None]]
        for kc in range(TAPS):
            value = shifted[kc, plane + kz]
            for b, index in ((0, index0), (1, index1)):
                taken = rows_at(value, index)
                if kc < 2:
                    corner[b][kc] = taken
                else:
                    corner[b][kc % 2] = jnp.where(picks[kc][0], taken, corner[b][kc % 2])
        flat = corner[0] + corner[1]
        if kz < 2:
            planes[kz] = flat
        else:
            mask = picks[kz][1]
            planes[kz % 2] = [jnp.where(mask, new, old) for new, old in zip(flat, planes[kz % 2])]
    parts = []
    for e0, o0, e1, o1 in planes:
        parts.append(
            weight0 * (col_e * e0 + col_o * o0) + weight1 * (col_e * e1 + col_o * o1)
        )
    summed = dep_e * parts[0] + dep_o * parts[1]
    return summed.astype(bf16).astype(f32)


def move_columns(slab, shifted, start, step):
    rows, cols = slab.shape[1:]
    offsets = [k - SHIFT for k in range(TAPS) if k != SHIFT]
    matrix = shift_matrix(offsets, cols)
    block = slab[start : start + step]
    shifted[SHIFT, start : start + step] = block
    moved = jnp.dot(
        block.reshape(step * rows, cols).astype(bf16), matrix, preferred_element_type=f32
    )
    for number, offset in enumerate(offsets):
        shifted[offset + SHIFT, start : start + step] = moved[
            :, number * cols : (number + 1) * cols
        ].reshape(step, rows, cols)


def vmem_specs(count):
    return [pl.BlockSpec(memory_space=pltpu.VMEM)] * count


def local_call(kernel, name, outs, inputs, scratch, flops):
    return pl.pallas_call(
        kernel,
        out_shape=[jax.ShapeDtypeStruct(shape, f32) for shape in outs],
        in_specs=vmem_specs(inputs),
        out_specs=vmem_specs(len(outs)),
        scratch_shapes=[pltpu.VMEM(shape, f32) for shape in scratch],
        compiler_params=pltpu.CompilerParams(vmem_limit_bytes=VMEM_LIMIT),
        cost_estimate=pl.CostEstimate(flops=flops, bytes_accessed=8_000_000, transcendentals=0),
        name=name,
    )


def slice_fields(shifts, fractions, z):
    return [shifts[axis, z] for axis in range(3)] + [
        fractions[axis, z].astype(f32) for axis in range(3)
    ]


def place_of_shard(me, shard, members):
    apart = me ^ shard
    quarter = members // PEERS
    peer = apart & (PEERS - 1)
    block = sum(jnp.where(peer == k, c, 0) for c, k in enumerate(ORDER))
    return block * quarter + mirrored(apart // PEERS, quarter)


def build_copy(share, rows, cols):
    def kernel(template, mine):
        mine[...] = template[...]

    return pl.pallas_call(
        kernel,
        out_shape=jax.ShapeDtypeStruct((share, rows, cols), bf16),
        in_specs=vmem_specs(1),
        out_specs=vmem_specs(1)[0],
        compiler_params=pltpu.CompilerParams(vmem_limit_bytes=VMEM_LIMIT),
        cost_estimate=pl.CostEstimate(flops=1_000, bytes_accessed=50_000, transcendentals=0),
        name="own_share",
    )


def build_pack(depth, rows, cols):
    def kernel(shifts, fractions, subjects, near, far, whole, parts, done):
        odd = lax.axis_index("gz") % 2 == 1
        copies = []
        for end, start in enumerate((0, depth - EDGE)):
            at = pl.ds(start, EDGE)
            copies.append(pltpu.make_async_copy(shifts.at[:, at], whole.at[end], done.at[3 * end]))
            copies.append(
                pltpu.make_async_copy(fractions.at[:, at], parts.at[end, 0:3], done.at[3 * end + 1])
            )
            copies.append(
                pltpu.make_async_copy(subjects.at[at], parts.at[end, 3], done.at[3 * end + 2])
            )
        for copy in copies:
            copy.start()
        for copy in copies:
            copy.wait()
        for axis in range(7):
            low, high = [
                (whole[end, axis] if axis < 3 else parts[end, axis - 3]).astype(f32)
                for end in range(2)
            ]
            near[axis] = jnp.where(odd, low, high).astype(bf16)
            far[axis] = jnp.where(odd, high, low).astype(bf16)

    message = jax.ShapeDtypeStruct((7, EDGE, rows, cols), bf16)
    return pl.pallas_call(
        kernel,
        out_shape=[message, message],
        in_specs=[pl.BlockSpec(memory_space=pl.ANY)] * 3,
        out_specs=vmem_specs(2),
        scratch_shapes=[
            pltpu.VMEM((2, 3, EDGE, rows, cols), jnp.int32),
            pltpu.VMEM((2, 4, EDGE, rows, cols), bf16),
            pltpu.SemaphoreType.DMA((6,)),
        ],
        compiler_params=pltpu.CompilerParams(vmem_limit_bytes=60 * 1024 * 1024),
        cost_estimate=pl.CostEstimate(flops=1_000_000, bytes_accessed=2_000_000, transcendentals=0),
        name="pack",
    )


def peer_shard(i, me, share, members, first):
    quarter = members // PEERS
    block = i // share
    return (me ^ (first + block // quarter + PEERS * (block % quarter))) * share + i % share


def end_slices(depth):
    return [*range(SHIFT), *range(depth - SHIFT - 1, depth)]


def build_inner_warp(depth, rows, cols, members):
    share = depth // members
    away = depth - depth // PEERS
    front, count = SHIFT, depth + 2 * SHIFT + 2

    def kernel(pieces, shifts, fractions, subjects, sent, send, shifted, slab):
        me = lax.axis_index("subj")
        quarter = members // PEERS
        slab[0:front] = jnp.zeros((front, rows, cols), f32)
        slab[front + depth : count] = jnp.zeros((count - front - depth, rows, cols), f32)
        for k in range(members):
            shard = me ^ (ORDER[k // quarter] + PEERS * mirrored(k % quarter, quarter))
            slab[pl.ds(front + shard * share, share)] = pieces[k * share : (k + 1) * share].astype(f32)
        for start in range(0, count, count // 2):
            move_columns(slab, shifted, start, count // 2)

        def body(i, carry):
            z = peer_shard(i, me, share, members, 1)
            out = warp_slice(shifted, front + z - SHIFT, *slice_fields(shifts, fractions, z))
            sent[i] = out
            send[i] = subjects[z].astype(f32) - out
            return carry

        lax.fori_loop(0, away, body, 0, unroll=6)

    part = (away, rows, cols)
    return local_call(
        kernel, "inner_warp", [part, part, (TAPS, count, rows, cols)], 4,
        [(count, rows, cols)], 1_000_000_000,
    )


def build_end_warp(depth, rows, cols, members, groups):
    share = depth // members
    quarter, kept = members // PEERS, depth // PEERS
    away = depth - kept
    inner = SHIFT + EDGE
    planes = HALO + inner

    def kernel(
        low_t, high_t, near_t, far_t, shifts, fractions, subjects, send_in, *outs_and_scratch
    ):
        *sends, ends, shifted, slab = outs_and_scratch
        odd = lax.axis_index("gz") % 2 == 1
        me = lax.axis_index("subj")
        inside = has_far(lax.axis_index("gz"), groups)
        near, far = near_t[...].astype(f32), jnp.where(inside, far_t[...].astype(f32), 0.0)
        slab[0:HALO] = jnp.where(odd, near, far)
        slab[HALO:planes] = low_t[0:inner].astype(f32)
        slab[planes : planes + inner] = high_t[HALO - inner : HALO].astype(f32)
        slab[planes + inner : 2 * planes] = jnp.where(odd, far, near)
        move_columns(slab, shifted, 0, 2 * planes)
        for number, send in enumerate(sends):
            send[...] = send_in[number * kept : (number + 1) * kept]
        for number, z in enumerate(end_slices(depth)):
            plane = HALO + z if z < SHIFT else 2 * planes - HALO - depth + z
            out = warp_slice(shifted, plane - SHIFT, *slice_fields(shifts, fractions, z))
            ends[number] = out
            residual = subjects[z].astype(f32) - out
            apart = me ^ (z // share)
            index = (apart // PEERS) * share + z % share
            for k, send in enumerate(sends, 1):

                @pl.when(apart % PEERS == k)
                def _():
                    send[index] = residual

    part = (kept, rows, cols)
    count = len(end_slices(depth))
    return local_call(
        kernel, "end_warp",
        [part] * (PEERS - 1) + [(count, rows, cols), (TAPS, 2 * planes, rows, cols)], 8,
        [(2 * planes, rows, cols)], 300_000_000,
    )


def build_rest_warp(depth, rows, cols, members, groups):
    share = depth // members
    kept = depth // PEERS
    planes = HALO + SHIFT + EDGE

    def kernel(
        moved, moved_ends, sent, ends, near_m, far_m, shifts, fractions, subjects, warped, keep
    ):
        me = lax.axis_index("subj")
        odd = lax.axis_index("gz") % 2 == 1
        inside = has_far(lax.axis_index("gz"), groups)

        def body(i, carry):
            z = peer_shard(i, me, share, members, 0)
            out = warp_slice(moved, z, *slice_fields(shifts, fractions, z))
            warped[EDGE + z] = out
            keep[i] = subjects[z].astype(f32) - out
            for part in range(PEERS - 1):
                number = part * kept + i
                warped[EDGE + peer_shard(number, me, share, members, 1)] = sent[number]
            return carry

        lax.fori_loop(0, kept, body, 0, unroll=4)
        for number, z in enumerate(end_slices(depth)):
            out = ends[number]
            warped[EDGE + z] = out
            apart = me ^ (z // share)

            @pl.when(apart % PEERS == 0)
            def _():
                keep[(apart // PEERS) * share + z % share] = subjects[z].astype(f32) - out

        def outside(z, carry):
            for low in (True, False):
                fields = []
                for axis in range(6):
                    one = near_m[axis, z].astype(f32)
                    two = jnp.where(inside, far_m[axis, z].astype(f32), 0.0)
                    field = jnp.where(odd, one, two) if low else jnp.where(odd, two, one)
                    fields.append(field.astype(jnp.int32) if axis < 3 else field)
                plane = HALO - EDGE + z if low else 2 * planes - HALO + z
                warped[z if low else depth + EDGE + z] = warp_slice(
                    moved_ends, plane - SHIFT, *fields
                )
            return carry

        lax.fori_loop(0, EDGE, outside, 0, unroll=2)

    return local_call(
        kernel, "rest_warp", [(depth + 2 * EDGE, rows, cols), (kept, rows, cols)], 9, [],
        600_000_000,
    )


def band(cols, radius):
    apart = jnp.abs(
        lax.broadcasted_iota(jnp.int32, (cols, cols), 0)
        - lax.broadcasted_iota(jnp.int32, (cols, cols), 1)
    )
    return (apart <= radius).astype(f32)


def column_difference(cols):
    apart = lax.broadcasted_iota(jnp.int32, (cols, cols), 0) - lax.broadcasted_iota(
        jnp.int32, (cols, cols), 1
    )
    return jnp.where(apart == 1, 0.5, jnp.where(apart == -1, -0.5, 0.0)).astype(f32)


def gauss_columns(cols):
    apart = jnp.abs(
        lax.broadcasted_iota(jnp.int32, (cols, cols), 0)
        - lax.broadcasted_iota(jnp.int32, (cols, cols), 1)
    )
    result = jnp.zeros((cols, cols), f32)
    for k, tap in enumerate(GAUSS):
        result = jnp.where(apart == k, f32(tap), result)
    return result


def split(value):
    high = value.astype(bf16)
    return high, (value - high.astype(f32)).astype(bf16)


def take_rows(value, index):
    return jnp.take_along_axis(value, index, axis=0, mode="promise_in_bounds")


def row_window(value, row):
    first = row < WIN
    half = value + take_rows(value, row ^ 1)
    half = half + take_rows(half, row ^ 2)
    outer = jnp.clip(jnp.where(first, row - 1, row + 1), 0, 2 * WIN - 1)
    outer_two = jnp.clip(jnp.where(first, row - 2, row + 2), 0, 2 * WIN - 1)
    reach = jnp.where(first, row, 2 * WIN - 1 - row)
    across = take_rows(value, row ^ WIN) + jnp.where(
        reach >= 1, take_rows(value, outer ^ WIN), 0.0
    )
    return half + across + jnp.where(reach >= 2, take_rows(across, outer_two), 0.0)


def z_windows(load, count):
    x = [load(k) for k in range(count + 2 * WIN)]
    two = [x[k] + x[k + 1] for k in range(count + 2 * WIN - 1)]
    four = [two[k] + two[k + 2] for k in range(count + 2 * WIN - 3)]
    return [four[k] + four[k + 4] + x[k + 8] for k in range(count)]


STEP = 8
CHUNK = 16
PART = 32
SCALE = 1.0 / float((2 * WIN + 1) ** 3)


def flat(value):
    return value.reshape(-1, value.shape[-1])


def square_columns(product, twice):
    pair = jnp.concatenate(split(product), axis=1)
    return jnp.dot(pair, twice, preferred_element_type=f32)


def build_image(depth, rows, cols, groups):
    ext, mid = depth + 2 * EDGE, depth + 2 * SMOOTH

    def kernel(near_m, far_m, subjects, image, mean, variance, boxes):
        odd = lax.axis_index("gz") % 2 == 1
        near = near_m[6].astype(f32)
        far = jnp.where(has_far(lax.axis_index("gz"), groups), far_m[6].astype(f32), 0.0)
        image[0:EDGE] = jnp.where(odd, near, far)
        image[EDGE : EDGE + depth] = subjects[...].astype(f32)
        image[EDGE + depth : ext] = jnp.where(odd, far, near)
        box = band(cols, WIN).astype(bf16)
        twice = jnp.concatenate([box, box], axis=0)

        def columns(i, carry):
            at = pl.ds(i * CHUNK, CHUNK)
            two = flat(image[at])
            results = [
                jnp.dot(two.astype(bf16), box, preferred_element_type=f32),
                square_columns(two * two, twice),
            ]
            for field, result in enumerate(results):
                boxes[field, at] = result.reshape(CHUNK, rows, cols)
            return carry

        lax.fori_loop(0, ext // CHUNK, columns, 0, unroll=True)
        row = lax.broadcasted_iota(jnp.int32, (rows, cols), 0)

        def local(i, carry):
            start = i * STEP
            one, two = [
                [row_window(v, row) * SCALE for v in z_windows(lambda k: boxes[f, start + k], STEP)]
                for f in range(2)
            ]
            for k in range(STEP):
                mean[start + k] = one[k]
                variance[start + k] = two[k] - one[k] * one[k]
            return carry

        lax.fori_loop(0, mid // STEP, local, 0, unroll=True)

    return local_call(
        kernel, "image",
        [(ext, rows, cols), (mid, rows, cols), (mid, rows, cols)], 3,
        [(2, ext, rows, cols)], 400_000_000,
    )


def build_force(depth, rows, cols, groups):
    ext, mid = depth + 2 * EDGE, depth + 2 * SMOOTH

    def kernel(warped, image, mean, variance, force, boxes, slope):
        box = band(cols, WIN)
        first = jnp.concatenate([box, column_difference(cols)], axis=1).astype(bf16)
        box = box.astype(bf16)
        twice = jnp.concatenate([box, box], axis=0)

        def columns(i, carry):
            at = pl.ds(i * CHUNK, CHUNK)
            one, two = flat(warped[at]), flat(image[at])
            both = jnp.dot(one.astype(bf16), first, preferred_element_type=f32)
            results = [both[:, :cols], square_columns(one * one, twice), square_columns(one * two, twice)]
            for field, result in enumerate(results):
                boxes[field, at] = result.reshape(CHUNK, rows, cols)
            slope[at] = both[:, cols:].reshape(CHUNK, rows, cols)
            return carry

        lax.fori_loop(0, ext // CHUNK, columns, 0, unroll=True)
        row = lax.broadcasted_iota(jnp.int32, (rows, cols), 0)

        def local(i, carry):
            start = i * STEP
            means = [
                [row_window(v, row) * SCALE for v in z_windows(lambda k: boxes[f, start + k], STEP)]
                for f in range(3)
            ]
            for k in range(STEP):
                mi, mii, mij = [field[k] for field in means]
                mj, var_j = mean[start + k], variance[start + k]
                at = start + k + WIN
                centre = warped[at]
                var_i = mii - mi * mi
                cov = mij - mi * mj
                factor = (image[at] - mj - cov / (var_i + epsilon) * (centre - mi)) / jnp.sqrt(
                    var_i * var_j + epsilon
                )
                grad_z = 0.5 * (warped[at + 1] - warped[at - 1])
                below = jnp.where(row < rows - 1, pltpu.roll(centre, rows - 1, 0), 0.0)
                above = jnp.where(row > 0, pltpu.roll(centre, 1, 0), 0.0)
                force[0, start + k] = factor * grad_z
                force[1, start + k] = factor * (0.5 * (below - above))
                force[2, start + k] = factor * slope[at]
            return carry

        lax.fori_loop(0, mid // STEP, local, 0, unroll=True)

        @pl.when(lax.axis_index("gz") == 0)
        def _():
            force[:, 0:SMOOTH] = jnp.zeros((3, SMOOTH, rows, cols), f32)

        @pl.when(lax.axis_index("gz") == groups - 1)
        def _():
            force[:, mid - SMOOTH : mid] = jnp.zeros((3, SMOOTH, rows, cols), f32)

    return local_call(
        kernel, "force", [(3, mid, rows, cols)], 4,
        [(3, ext, rows, cols), (ext, rows, cols)], 1_000_000_000,
    )


def build_smooth(depth, rows, cols):
    chunks = depth // PART

    def kernel(force, velocity, padded, result, done):
        g_high, g_low = split(gauss_columns(cols))
        g_all = jnp.concatenate(
            [
                jnp.concatenate([g_high, g_low], axis=1),
                jnp.concatenate([g_high, jnp.zeros_like(g_low)], axis=1),
            ],
            axis=0,
        )
        padded[...] = jnp.zeros(padded.shape, f32)

        def sent(i):
            at = pl.ds(i * PART, PART)
            return pltpu.make_async_copy(result.at[:, at], velocity.at[:, at], done.at[i])

        def finish(i, carry):
            start = i * PART
            for axis in range(3):
                x = [force[axis, start + k] for k in range(PART + 2 * SMOOTH)]
                for k in range(PART):
                    value = GAUSS[0] * x[k + SMOOTH]
                    for d in range(1, SMOOTH + 1):
                        value = value + GAUSS[d] * (x[k + SMOOTH - d] + x[k + SMOOTH + d])
                    padded[axis, k, SMOOTH : SMOOTH + rows] = value
                highs, lows = [], []
                for k in range(0, PART, 2):
                    both = []
                    for n in (k, k + 1):
                        value = GAUSS[0] * padded[axis, n, SMOOTH : SMOOTH + rows]
                        for d in range(1, SMOOTH + 1):
                            value = value + GAUSS[d] * (
                                padded[axis, n, SMOOTH - d : SMOOTH - d + rows]
                                + padded[axis, n, SMOOTH + d : SMOOTH + d + rows]
                            )
                        both.append(value)
                    high, low = split(jnp.concatenate(both, axis=0))
                    highs.append(high)
                    lows.append(low)
                pair = jnp.concatenate(
                    [jnp.concatenate(highs, axis=0), jnp.concatenate(lows, axis=0)], axis=1
                )
                mixed = jnp.dot(pair, g_all, preferred_element_type=f32)
                result[axis, pl.ds(start, PART)] = (mixed[:, :cols] + mixed[:, cols:]).reshape(
                    PART, rows, cols
                )
            sent(i).start()
            return carry

        lax.fori_loop(0, chunks, finish, 0, unroll=True)
        for i in range(chunks):
            sent(i).wait()

    return pl.pallas_call(
        kernel,
        out_shape=[jax.ShapeDtypeStruct((3, depth, rows, cols), f32)],
        in_specs=vmem_specs(1),
        out_specs=[pl.BlockSpec(memory_space=pl.ANY)],
        scratch_shapes=[
            pltpu.VMEM((3, PART, rows + 2 * SMOOTH, cols), f32),
            pltpu.VMEM((3, depth, rows, cols), f32),
            pltpu.SemaphoreType.DMA((chunks,)),
        ],
        compiler_params=pltpu.CompilerParams(vmem_limit_bytes=VMEM_LIMIT),
        cost_estimate=pl.CostEstimate(flops=600_000_000, bytes_accessed=8_000_000, transcendentals=0),
        name="smooth",
    )


def per_device(template, subjects, shifts, fractions):
    groups = lax.axis_size("gz")
    members = lax.axis_size("subj")
    subject_count, depth, rows, cols = subjects.shape
    share = depth // members
    reach = -(-HALO // share)
    me = lax.axis_index("subj")
    bits = bits_of(members)[2:]
    subject, shift, fraction = subjects[0], shifts[0], fractions[0]

    arrived = swap(template, "subj", bits[-1])
    mine = build_copy(share, rows, cols)(template)
    to_near, to_far = build_pack(depth, rows, cols)(shift, fraction, subject)
    pieces = jnp.concatenate([mine, arrived], axis=0)
    pieces, to_near, to_far = lax.optimization_barrier((pieces, to_near, to_far))
    near_m, far_m = swap_near(to_near, "gz"), swap_far(to_far, "gz")
    for bit in bits[-2::-1]:
        pieces = jnp.concatenate([pieces, swap(pieces, "subj", bit)], axis=0)
    pieces = jnp.concatenate(
        [pieces] + [swap(pieces, "subj", k) for k in ORDER[1:]], axis=0
    )

    def shares(numbers):
        starts = [place_of_shard(me, number, members) * share for number in numbers]
        return jnp.concatenate(
            [lax.dynamic_slice_in_dim(pieces, start, share, 0) for start in starts], axis=0
        )

    low_t = shares(range(reach))[:HALO]
    high_t = shares(range(members - reach, members))[-HALO:]
    to_near, to_far = at_ends("gz", low_t, high_t)
    near_t, far_t = swap_near(to_near, "gz"), swap_far(to_far, "gz")

    sent, send, moved = build_inner_warp(depth, rows, cols, members)(pieces, shift, fraction, subject)
    *sends, ends, moved_ends = build_end_warp(depth, rows, cols, members, groups)(
        low_t, high_t, near_t, far_t, shift, fraction, subject, send
    )

    parts = [swap(sends[k - 1], "subj", k) for k in (3, 1, 2)]
    warped, keep = build_rest_warp(depth, rows, cols, members, groups)(
        moved, moved_ends, sent, ends, near_m, far_m, shift, fraction, subject
    )
    near_m, far_m, subject, warped = lax.optimization_barrier((near_m, far_m, subject, warped))
    image, mean, variance = build_image(depth, rows, cols, groups)(near_m, far_m, subject)
    (force,) = build_force(depth, rows, cols, groups)(warped, image, mean, variance)
    *parts, force = lax.optimization_barrier((*parts, force))
    keep = keep + parts[0] + parts[1] + parts[2]
    for bit in bits:
        pairs = keep.reshape((-1, 2, share) + keep.shape[1:])
        keep, send = [pairs[:, part].reshape((-1,) + keep.shape[1:]) for part in (0, 1)]
        keep = keep + swap(send, "subj", bit)
    (velocity,) = build_smooth(depth, rows, cols)(force)
    template_force = keep * (1.0 / math.sqrt(subject_count * members))
    return (velocity[None], template_force)


def solution(mesh):
    placed = (
        P(("gz", "subj"), None, None),
        P("subj", "gz", None, None),
        P("subj", None, "gz", None, None),
        P("subj", None, "gz", None, None),
    )
    return jax.shard_map(
        per_device,
        mesh=mesh,
        in_specs=placed,
        out_specs=(P("subj", None, "gz", None, None), P(("gz", "subj"), None, None)),
        check_vma=False,
    )
```
